128 devices in a mesh: slot: 4 (over y), region: 32 (over z, x, core).
Axes of the slice: x: 4, y: 4, z: 4, core: 2. Of those that a mesh axis runs over, the one named last changes fastest.
Arguments:
- residual: float32 [4, 2, 685, 16384], P('slot', None, None, 'region'), may hold values from -32 to 32
- perturb: bfloat16 [4, 64, 685, 4096], P('slot', None, None, 'region'), may hold values from -3 to 3
- vertical_modes: float32 [685, 10], replicated, may hold values from -0.21875 to 0.21875
- column_weight: float32 [16384], P('region'), may hold values from 0.5 to 1.5
- owner_table: int32 [16384, 1], replicated, may hold values from 0 to 31; in each aligned block of 512 rows (0 to 511, 512 to 1023, ...) at most 32 rows name the same one
- column_map: int32 [16384], replicated, may hold values from 0 to 127
Outputs:
- hess_product: float32 [4, 2, 685, 16384], P('slot', None, None, 'region')
- step_length: float32 [2], replicated
- next_residual: float32 [4, 2, 685, 16384], P('slot', None, None, 'region')
The draws below stay inside these ranges and needn't reach their ends.
Inputs may be any that keep to these rules, and one draw needn't show every extreme that they name: `owner_table`: among the 512 fine columns of one region, at most 32 name the same owner, a bound that some block reaches.
All inputs are finite; a program needn't handle non-finite values.
Results may differ from the reference program's by a relative error of at most 0.004.
Values may be sent and summed in bfloat16 or wider, within the bound.
A program may use at most 128 MiB of HBM per device.

```python
import math
import jax
import jax.numpy as jnp
import numpy as np
from jax import lax

MEMBERS = 64
VERT_MODES = 10
VECTORS = 2
FINE_DEV = 512
LON_DEV = 16
LAT_ROWS = 8
FEATURES = 685
TIME_SLOTS = 4
FINE_ALL = 16384
LON_ALL = 512
COARSE_ALL = 4096
CAPACITY = 32
N_REGION = 32


def draw_residual(key, part):
    base_key = jax.random.fold_in(key, 11)
    rough_key = jax.random.fold_in(key, 12)
    common_key = jax.random.fold_in(key, 14)
    slot_key = jax.random.fold_in(key, 15)
    full_shape = (TIME_SLOTS, VECTORS, FEATURES, FINE_ALL)
    column_rise = 1.0 + 2.0 * jnp.arange(FINE_ALL, dtype=jnp.float32) / FINE_ALL
    slot_factor = jnp.exp(jax.random.uniform(slot_key, (TIME_SLOTS,), jnp.float32, math.log(0.7), math.log(1.4)))
    slot_rise = (1.0 + 2.0 * jnp.arange(TIME_SLOTS, dtype=jnp.float32) / max(TIME_SLOTS - 1, 1)) * slot_factor
    roughness = jax.random.uniform(rough_key, (1, 1, 1, FINE_ALL), jnp.float32, 0.5, 2.0)
    common = jnp.clip(jax.random.normal(common_key, (1, VECTORS, FEATURES, 1), jnp.float32), -3.0, 3.0)
    base_draw = jnp.clip(jax.random.normal(base_key, full_shape, jnp.float32), -4.0, 4.0)
    values = (0.8 * common + base_draw * roughness) * column_rise[None, None, None, :] * slot_rise[:, None, None, None] / 3.0
    return jnp.clip(values, -32.0, 32.0)


def draw_perturb(key, part):
    shared_key = jax.random.fold_in(key, 21)
    own_key = jax.random.fold_in(key, 22)
    rough_key = jax.random.fold_in(key, 23)
    phase_key = jax.random.fold_in(key, 24)
    full_shape = (TIME_SLOTS, MEMBERS, FEATURES, COARSE_ALL)
    shared = jnp.clip(jax.random.normal(shared_key, (1, MEMBERS, FEATURES, 1), jnp.float32), -4.0, 4.0)
    own = jnp.clip(jax.random.normal(own_key, (TIME_SLOTS, MEMBERS, FEATURES, 1), jnp.float32), -4.0, 4.0)
    phase = jax.random.uniform(phase_key, (1, MEMBERS, 1, 1), jnp.float32, -math.pi, math.pi)
    longitude = (jnp.arange(COARSE_ALL, dtype=jnp.int32) // LAT_ROWS).astype(jnp.float32)
    wave = 1.0 + 0.5 * jnp.sin(2.0 * math.pi * longitude[None, None, None, :] / LON_ALL + phase)
    rough = jnp.clip(jax.random.normal(rough_key, full_shape, jnp.float32), -4.0, 4.0)
    values = 0.4 * (0.85 * shared + 0.5 * own) * wave + 0.35 * rough
    return jnp.clip(values, -3.0, 3.0).astype(jnp.bfloat16)


def place_ends(values, key, low, largest):
    longest = values.shape.index(max(values.shape))
    spots = []
    for shift in (0, 1):
        where = [jax.random.randint(jax.random.fold_in(key, axis), (), 0, length) for axis, length in enumerate(values.shape)]
        where[longest] = (where[longest] + shift) % values.shape[longest]
        spots.append(tuple(where))
    return values.at[spots[0]].set(low).at[spots[1]].set(largest)


def block_levels(key, dims, split, least, high):
    loudness, own = 1.0, jax.random.fold_in(key, 6)
    for dim, parts in split:
        heights = jnp.exp(jax.random.uniform(jax.random.fold_in(own, dim), (parts,), jnp.float32, least / len(split), high / len(split)))
        loudness = loudness * jnp.repeat(heights, dims[dim] // parts).reshape([-1 if axis == dim else 1 for axis in range(len(dims))])
    return loudness


def assign_block(key, own, number, rows, number_of, top, reach, lean):
    sequence = jax.random.permutation(key, number_of)
    crowded, usual = portions_of(number_of, rows * top, reach, lean, True), portions_of(number_of, rows * top, reach, lean, False)
    places = jnp.arange(number_of)

    def named(lengths, rotation):
        used = int((lengths > 0).sum())
        fixed = max(1, used // 4)
        passed = fixed + (places - fixed + rotation * (used - fixed)) % max(1, number_of - fixed)
        return jnp.zeros((number_of,), jnp.int32).at[sequence[jnp.where(places < fixed, places, passed)]].set(jnp.asarray(lengths, jnp.int32))

    lengths = jnp.where(number % 4 == 0, named(crowded, number // 4), named(usual, number - number // 4 - 1))
    mixed = jax.random.permutation(jax.random.fold_in(own, 3), number_of)
    source_of, taker = mixed[0:number_of // 2 * 2:2], mixed[1:number_of // 2 * 2:2]
    margin = jnp.minimum(lengths[source_of] - 1, reach - lengths[taker]) // 2
    margin = jnp.where((source_of == sequence[0]) | (taker == sequence[0]) | (lengths[taker] == 0), 0, jnp.maximum(margin, 0))
    passed = jax.random.randint(jax.random.fold_in(own, 4), (number_of // 2,), 0, 1 << 20) % (margin + 1)
    lengths = lengths.at[source_of].add(-passed).at[taker].add(passed)
    items = jnp.searchsorted(jnp.cumsum(lengths), jnp.arange(rows * top), side="right").astype(jnp.int32)
    listing = items.reshape(top, rows).T
    listing = listing[jax.random.permutation(jax.random.fold_in(own, 1), rows)]
    rotation = jax.random.randint(jax.random.fold_in(own, 2), (rows, 1), 0, top)
    return jnp.take_along_axis(listing, (jnp.arange(top)[None, :] + rotation) % top, axis=1)


def portions_of(amount, total, reach, lean, full):
    weights = [(1 << 20) // math.isqrt(grade ** lean) + 1 for grade in range(1, amount + 1)]
    largest = reach if full else min(reach, max(-(-total // amount), total * weights[0] // sum(weights)))
    least = 1 if total - largest >= amount - 1 else 0
    counts, rest = [largest] + [least] * (amount - 1), total - largest - least * (amount - 1)
    while rest > 0:
        candidates = [i for i in range(1, amount) if counts[i] < largest] or [i for i in range(1, amount) if counts[i] < reach]
        whole, budget = sum([weights[i] for i in candidates]), rest
        for i in candidates:
            extra = min(reach - counts[i], max(1, budget * weights[i] // whole), rest)
            counts[i] = counts[i] + extra
            rest = rest - extra
    return np.array(counts)


def bell_draw(key, shape, width, reach, kind=jnp.bfloat16):
    result = jax.random.normal(key, shape, jnp.float32) * width
    return jnp.minimum(jnp.maximum(result, -reach), reach).astype(kind)


def setup_inputs(seed: int = 0) -> dict:
    splits = jax.random.split(jax.random.key(seed), 7)
    residual = draw_residual(jax.random.fold_in(splits[6], 71), 0)
    perturb = draw_perturb(jax.random.fold_in(splits[6], 71), 0)
    vertical_modes = bell_draw(splits[2], (FEATURES, VERT_MODES), FEATURES ** -0.5, 0.21875, jnp.float32)
    column_weight = jnp.clip(0.5 + 1.0 * jax.random.uniform(splits[3], (FINE_ALL,), jnp.float32) ** block_levels(splits[3], (FINE_ALL,), ((0, 32),), -0.2, 0.2), 0.5, 1.5)
    owner_table_keys = jax.random.split(jax.random.fold_in(splits[4], 1), FINE_ALL // FINE_DEV)
    owner_table_turns = jax.random.permutation(jax.random.fold_in(splits[4], 3), FINE_ALL // FINE_DEV)
    owner_table = jax.vmap(lambda own, number: assign_block(jax.random.fold_in(splits[4], 2), own, number, FINE_DEV, N_REGION, 1, CAPACITY, 2))(owner_table_keys, owner_table_turns).reshape((FINE_ALL, 1))
    column_map = place_ends(jax.random.randint(splits[5], (FINE_ALL,), 0, LON_DEV * LAT_ROWS), jax.random.fold_in(splits[5], 1), 0, (LON_DEV * LAT_ROWS) - 1).astype(jnp.int32)
    return {"residual": residual, "perturb": perturb, "vertical_modes": vertical_modes, "column_weight": column_weight, "owner_table": owner_table, "column_map": column_map}


DIFFUSION_RATE = 0.2


def smooth(grid_vals):
    across = jnp.roll(grid_vals, 1, 0) + jnp.roll(grid_vals, -1, 0) - 2.0 * grid_vals
    lat_steps = grid_vals[:, 1:] - grid_vals[:, :-1]
    along = jnp.pad(lat_steps, ((0, 0), (0, 1), (0, 0))) - jnp.pad(lat_steps, ((0, 0), (1, 0), (0, 0)))
    return grid_vals + DIFFUSION_RATE * (across + along)


def reference(residual, perturb, vertical_modes, column_weight, owner_table, column_map):
    target = (owner_table[:, 0] * (LON_DEV * LAT_ROWS) + column_map).astype(jnp.int32)
    mode_width = VECTORS * VERT_MODES
    mode_rows = vertical_modes.T

    def forward(slot_args):
        slot_resid, members = slot_args
        weighted = (slot_resid * column_weight[None, None, :]).astype(jnp.bfloat16)
        weighted = lax.optimization_barrier(weighted).astype(jnp.float32)
        by_column = weighted.reshape(VECTORS * FEATURES, FINE_ALL).T
        coarse = jax.ops.segment_sum(by_column, target, num_segments=COARSE_ALL).T
        coarse = coarse.reshape(VECTORS, FEATURES, COARSE_ALL)
        mode_mixed = (mode_rows[None, :, :, None] * coarse[:, None]).astype(jnp.bfloat16)
        mode_mixed = mode_mixed.reshape(mode_width, FEATURES, COARSE_ALL)
        return jnp.einsum("kfc,jfc->ckj", members.astype(jnp.float32), mode_mixed.astype(jnp.float32),
                          precision=lax.Precision.HIGHEST)

    partial_value = lax.map(forward, (residual, perturb))
    summed = jnp.sum(partial_value, axis=0).reshape(LON_ALL, LAT_ROWS, MEMBERS * mode_width)
    once_smoothed = smooth(summed)
    twice_smoothed = smooth(once_smoothed)
    control_squares = jnp.sum((once_smoothed * once_smoothed).reshape(LON_ALL * LAT_ROWS, MEMBERS, VECTORS, VERT_MODES), axis=(0, 1, 3))
    smoothed = twice_smoothed.astype(jnp.bfloat16).reshape(COARSE_ALL, MEMBERS, mode_width)

    def backward(slot_args):
        slot_resid, members = slot_args
        projected = jnp.einsum("kfc,ckj->jfc", members.astype(jnp.float32), smoothed.astype(jnp.float32),
                               precision=lax.Precision.HIGHEST)
        projected = projected.reshape(VECTORS, VERT_MODES, FEATURES, COARSE_ALL)
        increment = jnp.sum(mode_rows[None, :, :, None] * projected, axis=1).astype(jnp.bfloat16)
        increment = lax.optimization_barrier(increment).astype(jnp.float32)
        fine_back = jnp.take(increment, target, axis=2)
        return slot_resid + fine_back * column_weight[None, None, :]

    hess_product = lax.map(backward, (residual, perturb))
    resid_norms = jnp.sum(residual * residual, axis=(0, 2, 3))
    step_length = resid_norms / (resid_norms + control_squares)
    next_residual = residual - step_length[None, :, None, None] * hess_product
    return (hess_product, step_length, next_residual)
```

```python
import jax
import jax.numpy as jnp
from jax import lax
from jax.experimental import pallas as pl
from jax.experimental.pallas import tpu as pltpu
from jax.sharding import PartitionSpec as P

MESH = pl.DeviceIdType.MESH
LAT_ROWS = 8
DIFFUSION_RATE = 0.2
F32 = jnp.float32
BF16 = jnp.bfloat16

REGIONS = 32
CAP = 32
SLOTS = 4
FINE = 512
COARSE = 128
FEAT = 685
FEAT_PAD = 688
WIDE = 1408
MEMBERS = 64
MODES = 10
ROWS = MODES * MEMBERS
SHARE = ROWS // SLOTS
OUT_CUT = 768
BACK_CUT = 640

NEAR_FIRST = (
    [(0, 1), (1, 0), (0, 3), (3, 0)],
    [(1, 1), (3, 3), (1, 3), (3, 1)],
    [(2, 0), (0, 2)],
    [(2, 1), (1, 2), (2, 3), (3, 2)],
    [(2, 2)],
)
HOPS = [(z, x, c) for group in NEAR_FIRST[::-1] for c in (0, 1) for z, x in group] + [(0, 0, 1)]


def smooth(cells, west_from, east_from):
    lane = lax.broadcasted_iota(jnp.int32, cells.shape, 1)
    row = lane % LAT_ROWS
    west = pltpu.roll(jnp.where(lane >= COARSE - LAT_ROWS, west_from, cells), LAT_ROWS, 1)
    east = pltpu.roll(jnp.where(lane < LAT_ROWS, east_from, cells), COARSE - LAT_ROWS, 1)
    south = pltpu.roll(cells, 1, 1)
    north = pltpu.roll(cells, COARSE - 1, 1)
    along = jnp.where(row > 0, south - cells, 0.0) + jnp.where(row < LAT_ROWS - 1, north - cells, 0.0)
    return cells + DIFFUSION_RATE * (west + east - 2.0 * cells + along)


def dot(a, b):
    return jnp.dot(a, b, preferred_element_type=F32)


def kernel(
    owners_ref,
    map_ref,
    weight_ref,
    modes_t_ref,
    modes_b_ref,
    resid_hbm,
    members_hbm,
    fine_ref,
    step_ref,
    resid,
    members,
    wide_rows,
    wide_cols,
    slot_hot_t,
    slot_hot,
    place,
    place_t,
    send_a,
    send_b,
    recv_a,
    recv_b,
    coarse,
    control,
    summed_in,
    edge_out,
    edge_in,
    shares,
    gathered,
    smoothed,
    total,
    total_t,
    back_a,
    back_b,
    home_a,
    home_b,
    norm,
    norm_in,
    norm_sum,
    norm_all,
    load_sem,
    out_send,
    out_recv,
    back_send,
    back_recv,
    sum_send,
    sum_recv,
    edge_send,
    edge_recv,
    share_send,
    share_recv,
    norm_send,
    norm_recv,
    last_send,
    last_recv,
):
    me = lax.axis_index("region")
    slot = lax.axis_index("slot")
    z, x, core = me // 8, (me // 2) % 4, me % 2

    def region_at(hop):
        dz, dx, dc = hop
        return (((z + dz) % 4) * 4 + (x + dx) % 4) * 2 + (core + dc) % 2

    partners = [region_at(h) for h in HOPS]
    load_resid = pltpu.make_async_copy(resid_hbm, resid, load_sem.at[0])
    load_resid.start()
    load_members = pltpu.make_async_copy(members_hbm, members, load_sem.at[1])
    load_members.start()

    barrier = pltpu.get_barrier_semaphore()
    for p in partners:
        pl.semaphore_signal(barrier, inc=1, device_id={"region": p}, device_id_type=MESH)
    for d in (1, 2, 3):
        pl.semaphore_signal(barrier, inc=1, device_id={"slot": (slot + d) % SLOTS}, device_id_type=MESH)

    own = owners_ref[pl.ds(me, 1), :]
    owner_hot = (lax.broadcasted_iota(jnp.int32, (REGIONS, FINE), 0) == own).astype(BF16)
    earlier = (
        lax.broadcasted_iota(jnp.int32, (FINE, FINE), 0) < lax.broadcasted_iota(jnp.int32, (FINE, FINE), 1)
    ).astype(BF16)
    before = dot(owner_hot, earlier)
    rank = jnp.sum(owner_hot.astype(F32) * before, axis=0, keepdims=True)
    my_slots = own * CAP + rank.astype(jnp.int32)
    for q in range(4):
        rows = pl.ds(q * 256, 256)
        hot = lax.broadcasted_iota(jnp.int32, (256, FINE), 0) + q * 256 == my_slots
        slot_hot_t[rows, :] = hot.astype(F32).astype(BF16)

    wide_rows[pl.ds(1373, WIDE - 1373), :] = jnp.zeros((WIDE - 1373, FINE), F32)
    index_row = (map_ref[pl.ds(me, 1), :] + 1).astype(F32)
    wide_rows[pl.ds(FEAT, 3), :] = jnp.broadcast_to(index_row, (3, FINE))
    load_resid.wait()
    norm[...] = jnp.zeros_like(norm)
    for v in range(2):
        field = resid[v]
        wide_rows[pl.ds(v * FEAT_PAD, FEAT), :] = field * weight_ref[...]
        by_col = jnp.sum(field * field, axis=0, keepdims=True)
        norm[pl.ds(v, 1), :] = by_col[:, 0:128] + by_col[:, 128:256] + by_col[:, 256:384] + by_col[:, 384:512]
    for q in range(4):
        wide_cols[pl.ds(q * 128, 128), :] = wide_rows[:, q * 128 : (q + 1) * 128].T.astype(BF16)

    pl.semaphore_wait(barrier, len(HOPS) + 3)

    def pack(out, left, matrix, depth_rows, width):
        def one(q, carry):
            got = dot(matrix[pl.ds(pl.multiple_of(q * 256, 256), 256), :], depth_rows[:, left : left + width])
            out[pl.ds(q * 8, 8)] = got.astype(BF16).reshape(8, CAP, width)
            return carry

        lax.fori_loop(0, 4, one, 0)

    def exchange(source, landing, chunk, send_sems, recv_sems):
        copies = []
        for i, p in enumerate(partners):
            copy = pltpu.make_async_remote_copy(
                src_ref=source.at[p],
                dst_ref=landing.at[me],
                send_sem=send_sems.at[chunk, i],
                recv_sem=recv_sems.at[chunk, i],
                device_id={"region": p},
                device_id_type=MESH,
            )
            copy.start()
            copies.append(copy)
        landing[me] = source[me]
        return copies

    pack(send_a, 0, slot_hot_t, wide_cols, OUT_CUT)
    out_copies = exchange(send_a, recv_a, 0, out_send, out_recv)
    pack(send_b, OUT_CUT, slot_hot_t, wide_cols, WIDE - OUT_CUT)
    out_copies_b = exchange(send_b, recv_b, 1, out_send, out_recv)

    slot_hot[...] = slot_hot_t[...].T
    total[...] = jnp.zeros_like(total)
    smoothed[...] = jnp.zeros_like(smoothed)
    load_members.wait()

    def contract(v):
        field = coarse[pl.ds(v * FEAT_PAD, FEAT), :]

        def pair(i, carry):
            halves = [(members[2 * i + e].astype(F32) * field).astype(BF16) for e in range(2)]
            got = dot(modes_t_ref[...], jnp.concatenate(halves, axis=1))
            got = got[0:16] + got[16:32]
            for e in range(2):
                control[pl.ds(v * ROWS + 2 * i + e, MODES, stride=MEMBERS), :] = got[
                    0:MODES, e * COARSE : (e + 1) * COARSE
                ]
            return carry

        lax.fori_loop(0, MEMBERS // 2, pair, 0)

    def share_rows(v, t):
        return pl.ds(pl.multiple_of(v * ROWS + t * SHARE, 8), SHARE)

    def sum_start(v):
        copies = []
        for d in (2, 1, 3):
            t = (slot + d) % SLOTS
            copy = pltpu.make_async_remote_copy(
                src_ref=control.at[share_rows(v, t)],
                dst_ref=summed_in.at[v, d - 1],
                send_sem=sum_send.at[v, d - 1],
                recv_sem=sum_recv.at[v, d - 1],
                device_id={"slot": t},
                device_id_type=MESH,
            )
            copy.start()
            copies.append(copy)
        return copies

    def edges_start(v):
        cells = control[share_rows(v, slot), :]
        for d in range(3):
            cells = cells + summed_in[v, d]
        shares[v] = cells
        lane = lax.broadcasted_iota(jnp.int32, (40, COARSE), 1)
        east = jnp.zeros((40, COARSE), F32)
        west = jnp.zeros((40, COARSE), F32)
        for g in range(4):
            part = cells[g * 40 : (g + 1) * 40]
            mine = lane // 16 == g
            east = jnp.where(mine, pltpu.roll(part, 16 * g + 16, 1), east)
            west = jnp.where(mine, pltpu.roll(part, 16 * g, 1) if g else part, west)
        edge_out[v, 0] = east
        edge_out[v, 1] = west
        copies = []
        for side, p in ((0, (me + 1) % REGIONS), (1, (me + REGIONS - 1) % REGIONS)):
            copy = pltpu.make_async_remote_copy(
                src_ref=edge_out.at[v, side],
                dst_ref=edge_in.at[v, side],
                send_sem=edge_send.at[v, side],
                recv_sem=edge_recv.at[v, side],
                device_id={"region": p},
                device_id_type=MESH,
            )
            copy.start()
            copies.append(copy)
        return copies

    def smooth_share(v):
        cells = shares[v]
        lane = lax.broadcasted_iota(jnp.int32, (SHARE, COARSE), 1)
        west = jnp.concatenate([pltpu.roll(edge_in[v, 0], 112 - 16 * g, 1) for g in range(4)], axis=0)
        east = jnp.concatenate(
            [pltpu.roll(edge_in[v, 1], 128 - 16 * g, 1) if g else edge_in[v, 1] for g in range(4)], axis=0
        )
        once = smooth(cells, west, east)
        west = jnp.where(lane < LAT_ROWS, cells, west)
        east = jnp.where(lane >= COARSE - LAT_ROWS, cells, east)
        twice = smooth(once, smooth(west, west, west), smooth(east, east, east))
        norm[pl.ds(2 + v, 1), :] = jnp.sum(once * once, axis=0, keepdims=True)
        smooth_bits = twice.astype(BF16)
        gathered[v, slot] = smooth_bits
        copies = []
        for d in (2, 1, 3):
            copy = pltpu.make_async_remote_copy(
                src_ref=gathered.at[v, slot],
                dst_ref=gathered.at[v, slot],
                send_sem=share_send.at[v, d - 1],
                recv_sem=share_recv.at[v, d - 1],
                device_id={"slot": (slot + d) % SLOTS},
                device_id_type=MESH,
            )
            copy.start()
            copies.append(copy)
        return copies

    def expand(v):
        for t in range(SLOTS):
            smoothed[pl.ds(t * SHARE, SHARE), :] = gathered[v, t].astype(F32)

        def pair(i, carry):
            halves = []
            for e in range(2):
                cells = smoothed[pl.ds(2 * i + e, 16, stride=MEMBERS), :].astype(BF16)
                halves.append(jnp.concatenate([cells, cells], axis=0))
            mixed = dot(modes_b_ref[...], jnp.concatenate(halves, axis=1))
            total[pl.ds(v * FEAT_PAD, FEAT), :] += (
                members[2 * i].astype(F32) * mixed[:, 0:COARSE]
                + members[2 * i + 1].astype(F32) * mixed[:, COARSE : 2 * COARSE]
            )
            return carry

        lax.fori_loop(0, MEMBERS // 2, pair, 0)


    def arrived(copies):
        for copy in copies:
            copy.wait_recv()

    def back_start(chunk):
        left, width = ((0, BACK_CUT), (BACK_CUT, WIDE - BACK_CUT))[chunk]
        out = (back_a, back_b)[chunk]
        total_t[:, left : left + width] = total[pl.ds(left, width), :].T.astype(BF16)
        pack(out, left, place, total_t, width)
        return exchange(out, (home_a, home_b)[chunk], chunk, back_send, back_recv)

    def fine_rows(chunk):
        left, width = ((0, BACK_CUT), (BACK_CUT, WIDE - BACK_CUT))[chunk]
        home = (home_a, home_b)[chunk][...].reshape(REGIONS * CAP, width)
        for q in range(4):
            got = dot(slot_hot[pl.ds(q * 128, 128), :], home)
            fine_ref[pl.ds(left, width), q * 128 : (q + 1) * 128] = got.T.astype(BF16)

    arrived(out_copies)
    sent = recv_a[...].reshape(REGIONS * CAP, OUT_CUT)
    near = sent[:, 640:768].astype(F32)
    lane = lax.broadcasted_iota(jnp.int32, (REGIONS * CAP, COARSE), 1)
    index = jnp.sum(jnp.where(lane == FEAT - 640, near, 0.0), axis=1, keepdims=True)
    hot = (lane + 1).astype(F32) == index
    place[...] = hot.astype(F32).astype(BF16)
    place_t[...] = place[...].T
    coarse[pl.ds(0, OUT_CUT), :] = dot(place_t[...], sent).T
    contract(0)
    sum_copies = sum_start(0)
    arrived(sum_copies)
    edge_copies = edges_start(0)
    arrived(edge_copies)
    share_copies = smooth_share(0)

    arrived(out_copies_b)
    coarse[pl.ds(OUT_CUT, WIDE - OUT_CUT), :] = dot(
        place_t[...], recv_b[...].reshape(REGIONS * CAP, WIDE - OUT_CUT)
    ).T
    contract(1)
    sum_copies_b = sum_start(1)

    arrived(share_copies)
    expand(0)
    back_copies = back_start(0)

    arrived(sum_copies_b)
    edge_copies_b = edges_start(1)
    arrived(edge_copies_b)
    share_copies_b = smooth_share(1)
    norm_copies = []
    for d in (2, 1, 3):
        copy = pltpu.make_async_remote_copy(
            src_ref=norm,
            dst_ref=norm_in.at[d - 1],
            send_sem=norm_send.at[d - 1],
            recv_sem=norm_recv.at[d - 1],
            device_id={"slot": (slot + d) % SLOTS},
            device_id_type=MESH,
        )
        copy.start()
        norm_copies.append(copy)
    arrived(share_copies_b)
    expand(1)
    back_copies_b = back_start(1)
    arrived(norm_copies)
    norm_sum[...] = norm[...] + norm_in[0] + norm_in[1] + norm_in[2]
    last_copies = []
    for i, p in enumerate(partners):
        copy = pltpu.make_async_remote_copy(
            src_ref=norm_sum,
            dst_ref=norm_all.at[me],
            send_sem=last_send.at[i],
            recv_sem=last_recv.at[i],
            device_id={"region": p},
            device_id_type=MESH,
        )
        copy.start()
        last_copies.append(copy)
    norm_all[me] = norm_sum[...]

    arrived(back_copies)
    fine_rows(0)
    arrived(last_copies)
    sums = jnp.sum(jnp.sum(norm_all[...], axis=0), axis=1, keepdims=True)
    squares = jnp.broadcast_to(sums, (8, COARSE))
    step_ref[...] = squares / (squares + pltpu.roll(squares, 6, 0))
    arrived(back_copies_b)
    fine_rows(1)

    for copies in (
        out_copies,
        out_copies_b,
        sum_copies,
        sum_copies_b,
        edge_copies,
        edge_copies_b,
        share_copies,
        share_copies_b,
        norm_copies,
        last_copies,
        back_copies,
        back_copies_b,
    ):
        for copy in copies:
            copy.wait_send()


def per_device(residual, perturb, vertical_modes, column_weight, owner_table, column_map):
    vmem, dma = pltpu.VMEM, pltpu.SemaphoreType.DMA
    resid_part = residual[0]
    high = vertical_modes.astype(BF16)
    low = (vertical_modes - high.astype(F32)).astype(BF16)
    both = jnp.concatenate([jnp.pad(high, ((0, 0), (0, 6))), jnp.pad(low, ((0, 0), (0, 6)))], axis=1)
    whole = pl.BlockSpec(memory_space=pltpu.VMEM)
    anywhere = pl.BlockSpec(memory_space=pl.ANY)
    n = len(HOPS)
    fine, step = pl.pallas_call(
        kernel,
        out_shape=(
            jax.ShapeDtypeStruct((WIDE, FINE), BF16),
            jax.ShapeDtypeStruct((8, COARSE), F32),
        ),
        in_specs=[whole] * 5 + [anywhere] * 2,
        out_specs=(whole, whole),
        scratch_shapes=[
            vmem((2, FEAT, FINE), F32),
            vmem((MEMBERS, FEAT, COARSE), BF16),
            vmem((WIDE, FINE), F32),
            vmem((FINE, WIDE), BF16),
            vmem((REGIONS * CAP, FINE), BF16),
            vmem((FINE, REGIONS * CAP), BF16),
            vmem((REGIONS * CAP, COARSE), BF16),
            vmem((COARSE, REGIONS * CAP), BF16),
            vmem((REGIONS, CAP, OUT_CUT), BF16),
            vmem((REGIONS, CAP, WIDE - OUT_CUT), BF16),
            vmem((REGIONS, CAP, OUT_CUT), BF16),
            vmem((REGIONS, CAP, WIDE - OUT_CUT), BF16),
            vmem((WIDE, COARSE), F32),
            vmem((2 * ROWS, COARSE), F32),
            vmem((2, SLOTS - 1, SHARE, COARSE), F32),
            vmem((2, 2, 40, COARSE), F32),
            vmem((2, 2, 40, COARSE), F32),
            vmem((2, SHARE, COARSE), F32),
            vmem((2, SLOTS, SHARE, COARSE), BF16),
            vmem((16 * MEMBERS, COARSE), F32),
            vmem((WIDE, COARSE), F32),
            vmem((COARSE, WIDE), BF16),
            vmem((REGIONS, CAP, BACK_CUT), BF16),
            vmem((REGIONS, CAP, WIDE - BACK_CUT), BF16),
            vmem((REGIONS, CAP, BACK_CUT), BF16),
            vmem((REGIONS, CAP, WIDE - BACK_CUT), BF16),
            vmem((8, COARSE), F32),
            vmem((SLOTS - 1, 8, COARSE), F32),
            vmem((8, COARSE), F32),
            vmem((REGIONS, 8, COARSE), F32),
            dma((2,)),
            dma((2, n)),
            dma((2, n)),
            dma((2, n)),
            dma((2, n)),
            dma((2, 3)),
            dma((2, 3)),
            dma((2, 2)),
            dma((2, 2)),
            dma((2, 3)),
            dma((2, 3)),
            dma((3,)),
            dma((3,)),
            dma((n,)),
            dma((n,)),
        ],
        compiler_params=pltpu.CompilerParams(
            collective_id=0, has_side_effects=True, vmem_limit_bytes=60 * 2**20
        ),
        name="hessian",
    )(
        owner_table.reshape(REGIONS, FINE),
        column_map.reshape(REGIONS, FINE),
        column_weight.reshape(1, FINE),
        both.T,
        both,
        resid_part,
        perturb[0],
    )
    increment = jnp.stack([fine[0:FEAT], fine[FEAT_PAD : FEAT_PAD + FEAT]]).astype(F32)
    product = resid_part + increment * column_weight[None, None, :]
    step_length = step[0:2, 0]
    next_residual = resid_part - step_length[:, None, None] * product
    return (product[None], step_length, next_residual[None])


def solution(mesh):
    in_specs = (
        P("slot", None, None, "region"),
        P("slot", None, None, "region"),
        P(),
        P("region"),
        P(),
        P(),
    )
    out_specs = (P("slot", None, None, "region"), P(), P("slot", None, None, "region"))
    return jax.shard_map(
        per_device, mesh=mesh, in_specs=in_specs, out_specs=out_specs, check_vma=False
    )
```

```python
import jax
import jax.numpy as jnp
from jax import lax
from jax.experimental import pallas as pl
from jax.experimental.pallas import tpu as pltpu
from jax.sharding import PartitionSpec as P

MESH = pl.DeviceIdType.MESH
LAT_ROWS = 8
DIFFUSION_RATE = 0.2
F32 = jnp.float32
BF16 = jnp.bfloat16

REGIONS = 32
CAP = 32
SLOTS = 4
FINE = 512
COARSE = 128
FEAT = 685
FEAT_PAD = 704
WIDE = 1408
MEMBERS = 64
MODES = 10
ROWS = MODES * MEMBERS
SHARE = ROWS // SLOTS
OUT_CUT = 768
BACK_CUT = 640
GROUP = 8
GROUPS = MEMBERS // GROUP
SPREAD = MODES * GROUP
STEP = 64

NEAR_FIRST = (
    [(0, 1), (1, 0), (0, 3), (3, 0)],
    [(1, 1), (3, 3), (1, 3), (3, 1)],
    [(2, 0), (0, 2)],
    [(2, 1), (1, 2), (2, 3), (3, 2)],
    [(2, 2)],
)
HOPS = [(z, x, c) for group in NEAR_FIRST[::-1] for c in (0, 1) for z, x in group] + [(0, 0, 1)]


def smooth(cells, west_from, east_from):
    lane = lax.broadcasted_iota(jnp.int32, cells.shape, 1)
    row = lane % LAT_ROWS
    west = pltpu.roll(jnp.where(lane >= COARSE - LAT_ROWS, west_from, cells), LAT_ROWS, 1)
    east = pltpu.roll(jnp.where(lane < LAT_ROWS, east_from, cells), COARSE - LAT_ROWS, 1)
    south = pltpu.roll(cells, 1, 1)
    north = pltpu.roll(cells, COARSE - 1, 1)
    along = jnp.where(row > 0, south - cells, 0.0) + jnp.where(row < LAT_ROWS - 1, north - cells, 0.0)
    return cells + DIFFUSION_RATE * (west + east - 2.0 * cells + along)


def dot(a, b):
    return jnp.dot(a, b, preferred_element_type=F32)


def kernel(
    owners_ref,
    map_ref,
    weight_ref,
    modes_ref,
    resid_hbm,
    members_hbm,
    fine_hbm,
    step_ref,
    resid,
    members,
    wide_rows,
    wide_cols,
    slot_hot_t,
    slot_hot,
    place,
    place_t,
    send_a,
    send_b,
    recv_a,
    recv_b,
    coarse,
    modes_rep,
    mixer,
    mixer_t,
    gathered_modes,
    mode_cells,
    control,
    summed_in,
    edge_out,
    edge_in,
    shares,
    gathered,
    total,
    total_t,
    back_a,
    back_b,
    home_a,
    home_b,
    fine,
    norm,
    norm_in,
    norm_sum,
    norm_all,
    load_sem,
    out_send,
    out_recv,
    back_send,
    back_recv,
    sum_send,
    sum_recv,
    edge_send,
    edge_recv,
    share_send,
    share_recv,
    norm_send,
    norm_recv,
    last_send,
    last_recv,
):
    me = lax.axis_index("region")
    slot = lax.axis_index("slot")
    z, x, core = me // 8, (me // 2) % 4, me % 2

    def region_at(hop):
        dz, dx, dc = hop
        return (((z + dz) % 4) * 4 + (x + dx) % 4) * 2 + (core + dc) % 2

    partners = [region_at(h) for h in HOPS]
    load_resid = [pltpu.make_async_copy(resid_hbm.at[:, v, :], resid.at[v], load_sem.at[v]) for v in range(2)]
    for copy in load_resid:
        copy.start()
    load_members = pltpu.make_async_copy(members_hbm, members.at[pl.ds(0, FEAT)], load_sem.at[2])
    load_members.start()

    barrier = pltpu.get_barrier_semaphore()
    for p in partners:
        pl.semaphore_signal(barrier, inc=1, device_id={"region": p}, device_id_type=MESH)
    for d in (1, 2, 3):
        pl.semaphore_signal(barrier, inc=1, device_id={"slot": (slot + d) % SLOTS}, device_id_type=MESH)

    mine = pl.ds(pl.multiple_of(me * FINE, FINE), FINE)
    own = owners_ref[:, mine]
    owner_hot = (lax.broadcasted_iota(jnp.int32, (REGIONS, FINE), 0) == own).astype(BF16)
    earlier = (
        lax.broadcasted_iota(jnp.int32, (FINE, FINE), 0) < lax.broadcasted_iota(jnp.int32, (FINE, FINE), 1)
    ).astype(BF16)
    before = dot(owner_hot, earlier)
    rank = jnp.sum(owner_hot.astype(F32) * before, axis=0, keepdims=True)
    my_slots = own * CAP + rank.astype(jnp.int32)
    for q in range(4):
        rows = pl.ds(q * 256, 256)
        hot = lax.broadcasted_iota(jnp.int32, (256, FINE), 0) + q * 256 == my_slots
        slot_hot_t[rows, :] = hot.astype(F32).astype(BF16)

    index_row = (map_ref[:, mine] + 1).astype(F32)
    spare = FEAT_PAD - FEAT
    wide_rows[pl.ds(FEAT, spare), :] = jnp.broadcast_to(index_row, (spare, FINE))
    wide_rows[pl.ds(FEAT_PAD + FEAT, spare), :] = jnp.zeros((spare, FINE), F32)
    norm[...] = jnp.zeros_like(norm)
    for v in range(2):
        load_resid[v].wait()
        field = resid[v]
        wide_rows[pl.ds(v * FEAT_PAD, FEAT), :] = field * weight_ref[...]
        by_col = jnp.sum(field * field, axis=0, keepdims=True)
        norm[pl.ds(v, 1), :] = by_col[:, 0:128] + by_col[:, 128:256] + by_col[:, 256:384] + by_col[:, 384:512]
    for q in range(4):
        wide_cols[pl.ds(q * 128, 128), :] = wide_rows[:, q * 128 : (q + 1) * 128].T.astype(BF16)

    pl.semaphore_wait(barrier, len(HOPS) + 3)

    def pack(out, left, matrix, depth_rows, width):
        def one(q, carry):
            got = dot(matrix[pl.ds(pl.multiple_of(q * 256, 256), 256), :], depth_rows[:, left : left + width])
            out[pl.ds(q * 8, 8)] = got.astype(BF16).reshape(8, CAP, width)
            return carry

        lax.fori_loop(0, 4, one, 0)

    def exchange(source, landing, chunk, send_sems, recv_sems):
        copies = []
        for i, p in enumerate(partners):
            copy = pltpu.make_async_remote_copy(
                src_ref=source.at[p],
                dst_ref=landing.at[me],
                send_sem=send_sems.at[chunk, i],
                recv_sem=recv_sems.at[chunk, i],
                device_id={"region": p},
                device_id_type=MESH,
            )
            copy.start()
            copies.append(copy)
        landing[me] = source[me]
        return copies

    pack(send_a, 0, slot_hot_t, wide_cols, OUT_CUT)
    out_copies = exchange(send_a, recv_a, 0, out_send, out_recv)
    pack(send_b, OUT_CUT, slot_hot_t, wide_cols, WIDE - OUT_CUT)
    out_copies_b = exchange(send_b, recv_b, 1, out_send, out_recv)

    slot_hot[...] = slot_hot_t[...].T
    members[pl.ds(FEAT, spare)] = jnp.zeros((spare, MEMBERS, COARSE), BF16)

    repeat = (
        lax.broadcasted_iota(jnp.int32, (SPREAD, MODES), 0) // GROUP
        == lax.broadcasted_iota(jnp.int32, (SPREAD, MODES), 1)
    ).astype(F32).astype(BF16)
    high = modes_ref[...].astype(BF16)
    low = (modes_ref[...] - high.astype(F32)).astype(BF16)
    modes_rep[...] = jnp.zeros_like(modes_rep)
    modes_rep[pl.ds(0, FEAT), :] = jnp.concatenate([dot(repeat, high), dot(repeat, low)], axis=0).T

    def mixer_step(i, carry):
        cut = (32, GROUP, 2 * SPREAD)
        rows = modes_rep[pl.ds(pl.multiple_of(i * 32, 32), 32), :]
        same = lax.broadcasted_iota(jnp.int32, cut, 1) == lax.broadcasted_iota(jnp.int32, cut, 2) % GROUP
        block = jnp.where(same, jnp.broadcast_to(rows[:, None, :], cut), 0.0).reshape(256, 2 * SPREAD)
        at = pl.ds(pl.multiple_of(i * 256, 256), 256)
        mixer[at, :] = block.astype(BF16)
        mixer_t[:, at] = block.T.astype(BF16)
        return carry

    lax.fori_loop(0, FEAT_PAD // 32, mixer_step, 0)
    load_members.wait()

    def contract(v):
        gathered_modes[...] = jnp.zeros_like(gathered_modes)

        def chunk(i, carry):
            field = coarse[pl.ds(pl.multiple_of(v * FEAT_PAD + i * STEP, STEP), STEP), :]
            cells = members[pl.ds(i * STEP, STEP)].astype(F32).reshape(STEP, GROUPS, GROUP, COARSE)
            product = cells * field[:, None, None, :]
            left = mixer_t[:, pl.ds(pl.multiple_of(i * STEP * GROUP, STEP * GROUP), STEP * GROUP)]
            for pair in range(GROUPS // 2):
                both = jnp.concatenate(
                    [product[:, 2 * pair + e].reshape(STEP * GROUP, COARSE) for e in range(2)], axis=1
                )
                top = both.astype(BF16)
                rest = (both - top.astype(F32)).astype(BF16)
                main = dot(left, top)
                gathered_modes[:, pair * 256 : (pair + 1) * 256] += (
                    main[0:SPREAD] + main[SPREAD:] + dot(left[0:SPREAD], rest)
                )
            return carry

        lax.fori_loop(0, FEAT_PAD // STEP, chunk, 0)
        for m in range(MODES):
            for g in range(GROUPS):
                control[pl.ds(v * ROWS + m * MEMBERS + g * GROUP, GROUP), :] = gathered_modes[
                    m * GROUP : (m + 1) * GROUP, g * COARSE : (g + 1) * COARSE
                ]

    def share_rows(v, t):
        return pl.ds(pl.multiple_of(v * ROWS + t * SHARE, 8), SHARE)

    def sum_start(v):
        copies = []
        for d in (2, 1, 3):
            t = (slot + d) % SLOTS
            copy = pltpu.make_async_remote_copy(
                src_ref=control.at[share_rows(v, t)],
                dst_ref=summed_in.at[v, d - 1],
                send_sem=sum_send.at[v, d - 1],
                recv_sem=sum_recv.at[v, d - 1],
                device_id={"slot": t},
                device_id_type=MESH,
            )
            copy.start()
            copies.append(copy)
        return copies

    def edges_start(v):
        cells = control[share_rows(v, slot), :]
        for d in range(3):
            cells = cells + summed_in[v, d]
        shares[v] = cells
        lane = lax.broadcasted_iota(jnp.int32, (40, COARSE), 1)
        east = jnp.zeros((40, COARSE), F32)
        west = jnp.zeros((40, COARSE), F32)
        for g in range(4):
            part = cells[g * 40 : (g + 1) * 40]
            mine = lane // 16 == g
            east = jnp.where(mine, pltpu.roll(part, 16 * g + 16, 1), east)
            west = jnp.where(mine, pltpu.roll(part, 16 * g, 1) if g else part, west)
        edge_out[v, 0] = east
        edge_out[v, 1] = west
        copies = []
        for side, p in ((0, (me + 1) % REGIONS), (1, (me + REGIONS - 1) % REGIONS)):
            copy = pltpu.make_async_remote_copy(
                src_ref=edge_out.at[v, side],
                dst_ref=edge_in.at[v, side],
                send_sem=edge_send.at[v, side],
                recv_sem=edge_recv.at[v, side],
                device_id={"region": p},
                device_id_type=MESH,
            )
            copy.start()
            copies.append(copy)
        return copies

    def smooth_share(v):
        cells = shares[v]
        lane = lax.broadcasted_iota(jnp.int32, (SHARE, COARSE), 1)
        west = jnp.concatenate([pltpu.roll(edge_in[v, 0], 112 - 16 * g, 1) for g in range(4)], axis=0)
        east = jnp.concatenate(
            [pltpu.roll(edge_in[v, 1], 128 - 16 * g, 1) if g else edge_in[v, 1] for g in range(4)], axis=0
        )
        once = smooth(cells, west, east)
        west = jnp.where(lane < LAT_ROWS, cells, west)
        east = jnp.where(lane >= COARSE - LAT_ROWS, cells, east)
        twice = smooth(once, smooth(west, west, west), smooth(east, east, east))
        norm[pl.ds(2 + v, 1), :] = jnp.sum(once * once, axis=0, keepdims=True)
        smooth_bits = twice.astype(BF16)
        gathered[v, slot] = smooth_bits
        copies = []
        for d in (2, 1, 3):
            copy = pltpu.make_async_remote_copy(
                src_ref=gathered.at[v, slot],
                dst_ref=gathered.at[v, slot],
                send_sem=share_send.at[v, d - 1],
                recv_sem=share_recv.at[v, d - 1],
                device_id={"slot": (slot + d) % SLOTS},
                device_id_type=MESH,
            )
            copy.start()
            copies.append(copy)
        return copies

    def expand(v):
        every = jnp.concatenate([gathered[v, t].astype(F32) for t in range(SLOTS)], axis=0)
        for g in range(GROUPS):
            cells = jnp.concatenate(
                [every[m * MEMBERS + g * GROUP : m * MEMBERS + (g + 1) * GROUP] for m in range(MODES)], axis=0
            ).astype(BF16)
            mode_cells[0:SPREAD, g * COARSE : (g + 1) * COARSE] = cells
            mode_cells[SPREAD:, g * COARSE : (g + 1) * COARSE] = cells

        def chunk(i, carry):
            left = mixer[pl.ds(pl.multiple_of(i * STEP * GROUP, STEP * GROUP), STEP * GROUP), :]
            cells = members[pl.ds(i * STEP, STEP)].astype(F32).reshape(STEP, GROUPS, GROUP, COARSE)
            sums = jnp.zeros((STEP, GROUP, COARSE), F32)
            for pair in range(GROUPS // 2):
                mixed = dot(left, mode_cells[:, pair * 256 : (pair + 1) * 256])
                for e in range(2):
                    part = mixed[:, e * COARSE : (e + 1) * COARSE].reshape(STEP, GROUP, COARSE)
                    sums = sums + cells[:, 2 * pair + e] * part
            at = pl.ds(pl.multiple_of(v * FEAT_PAD + i * STEP, STEP), STEP)
            total[at, :] = jnp.sum(sums, axis=1)
            return carry

        lax.fori_loop(0, FEAT_PAD // STEP, chunk, 0)

    def arrived(copies):
        for copy in copies:
            copy.wait_recv()

    def back_start(chunk):
        left, width = ((0, BACK_CUT), (BACK_CUT, WIDE - BACK_CUT))[chunk]
        out = (back_a, back_b)[chunk]
        total_t[:, left : left + width] = total[pl.ds(left, width), :].T.astype(BF16)
        pack(out, left, place, total_t, width)
        return exchange(out, (home_a, home_b)[chunk], chunk, back_send, back_recv)

    def fine_rows(chunk):
        left, width = ((0, BACK_CUT), (BACK_CUT, WIDE - BACK_CUT))[chunk]
        home = (home_a, home_b)[chunk][...].reshape(REGIONS * CAP, width)
        for q in range(4):
            got = dot(slot_hot[pl.ds(q * 128, 128), :], home)
            rows, cols = got.T, slice(q * 128, (q + 1) * 128)
            if chunk == 0:
                fine[0, 0:BACK_CUT, cols] = rows
            else:
                fine[0, BACK_CUT:FEAT, cols] = rows[0 : FEAT - BACK_CUT]
                fine[1, :, cols] = rows[FEAT_PAD - BACK_CUT : FEAT_PAD - BACK_CUT + FEAT]

    arrived(out_copies)
    sent = recv_a[...].reshape(REGIONS * CAP, OUT_CUT)
    near = sent[:, 640:768].astype(F32)
    lane = lax.broadcasted_iota(jnp.int32, (REGIONS * CAP, COARSE), 1)
    index = jnp.sum(jnp.where(lane == FEAT - 640, near, 0.0), axis=1, keepdims=True)
    hot = (lane + 1).astype(F32) == index
    place[...] = hot.astype(F32).astype(BF16)
    place_t[...] = place[...].T
    coarse[pl.ds(0, OUT_CUT), :] = dot(place_t[...], sent).T
    total[pl.ds(FEAT_PAD, FEAT_PAD), :] = jnp.zeros((FEAT_PAD, COARSE), F32)
    contract(0)
    sum_copies = sum_start(0)
    arrived(sum_copies)
    edge_copies = edges_start(0)
    arrived(edge_copies)
    share_copies = smooth_share(0)

    arrived(out_copies_b)
    coarse[pl.ds(OUT_CUT, WIDE - OUT_CUT), :] = dot(
        place_t[...], recv_b[...].reshape(REGIONS * CAP, WIDE - OUT_CUT)
    ).T
    contract(1)
    sum_copies_b = sum_start(1)

    arrived(share_copies)
    expand(0)
    back_copies = back_start(0)

    arrived(sum_copies_b)
    edge_copies_b = edges_start(1)
    arrived(edge_copies_b)
    share_copies_b = smooth_share(1)
    norm_copies = []
    for d in (2, 1, 3):
        copy = pltpu.make_async_remote_copy(
            src_ref=norm,
            dst_ref=norm_in.at[d - 1],
            send_sem=norm_send.at[d - 1],
            recv_sem=norm_recv.at[d - 1],
            device_id={"slot": (slot + d) % SLOTS},
            device_id_type=MESH,
        )
        copy.start()
        norm_copies.append(copy)
    arrived(share_copies_b)
    expand(1)
    back_copies_b = back_start(1)
    arrived(norm_copies)
    norm_sum[...] = norm[...] + norm_in[0] + norm_in[1] + norm_in[2]
    last_copies = []
    for i, p in enumerate(partners):
        copy = pltpu.make_async_remote_copy(
            src_ref=norm_sum,
            dst_ref=norm_all.at[me],
            send_sem=last_send.at[i],
            recv_sem=last_recv.at[i],
            device_id={"region": p},
            device_id_type=MESH,
        )
        copy.start()
        last_copies.append(copy)
    norm_all[me] = norm_sum[...]

    arrived(back_copies)
    fine_rows(0)
    arrived(last_copies)
    sums = jnp.sum(jnp.sum(norm_all[...], axis=0), axis=1, keepdims=True)
    squares = jnp.broadcast_to(sums, (8, COARSE))
    step_ref[...] = squares / (squares + pltpu.roll(squares, 6, 0))
    arrived(back_copies_b)
    fine_rows(1)
    stores = [
        pltpu.make_async_copy(fine.at[v], fine_hbm.at[:, v, :], load_sem.at[v])
        for v in range(2)
    ]
    for copy in stores:
        copy.start()
    for copy in stores:
        copy.wait()

    for copies in (
        out_copies,
        out_copies_b,
        sum_copies,
        sum_copies_b,
        edge_copies,
        edge_copies_b,
        share_copies,
        share_copies_b,
        norm_copies,
        last_copies,
        back_copies,
        back_copies_b,
    ):
        for copy in copies:
            copy.wait_send()


def last_step(resid_ref, increment_ref, weight_ref, step_ref, product_ref, next_ref):
    step = jnp.concatenate([step_ref[0:2, :]] * 4, axis=1)[None]
    product = resid_ref[...] + increment_ref[...] * weight_ref[...][None]
    product_ref[...] = product
    next_ref[...] = resid_ref[...] - step * product


def per_device(residual, perturb, vertical_modes, column_weight, owner_table, column_map):
    vmem, dma = pltpu.VMEM, pltpu.SemaphoreType.DMA
    resid_part = residual[0].transpose(1, 0, 2)
    weight = column_weight.reshape(1, FINE)
    whole = pl.BlockSpec(memory_space=pltpu.VMEM)
    anywhere = pl.BlockSpec(memory_space=pl.ANY)
    n = len(HOPS)
    increment, step = pl.pallas_call(
        kernel,
        out_shape=(
            jax.ShapeDtypeStruct((FEAT, 2, FINE), F32),
            jax.ShapeDtypeStruct((8, COARSE), F32),
        ),
        in_specs=[whole] * 4 + [anywhere] * 2,
        out_specs=(anywhere, whole),
        scratch_shapes=[
            vmem((2, FEAT, FINE), F32),
            vmem((FEAT_PAD, MEMBERS, COARSE), BF16),
            vmem((WIDE, FINE), F32),
            vmem((FINE, WIDE), BF16),
            vmem((REGIONS * CAP, FINE), BF16),
            vmem((FINE, REGIONS * CAP), BF16),
            vmem((REGIONS * CAP, COARSE), BF16),
            vmem((COARSE, REGIONS * CAP), BF16),
            vmem((REGIONS, CAP, OUT_CUT), BF16),
            vmem((REGIONS, CAP, WIDE - OUT_CUT), BF16),
            vmem((REGIONS, CAP, OUT_CUT), BF16),
            vmem((REGIONS, CAP, WIDE - OUT_CUT), BF16),
            vmem((WIDE, COARSE), F32),
            vmem((FEAT_PAD, 2 * SPREAD), F32),
            vmem((FEAT_PAD * GROUP, 2 * SPREAD), BF16),
            vmem((2 * SPREAD, FEAT_PAD * GROUP), BF16),
            vmem((SPREAD, GROUPS * COARSE), F32),
            vmem((2 * SPREAD, GROUPS * COARSE), BF16),
            vmem((2 * ROWS, COARSE), F32),
            vmem((2, SLOTS - 1, SHARE, COARSE), F32),
            vmem((2, 2, 40, COARSE), F32),
            vmem((2, 2, 40, COARSE), F32),
            vmem((2, SHARE, COARSE), F32),
            vmem((2, SLOTS, SHARE, COARSE), BF16),
            vmem((WIDE, COARSE), F32),
            vmem((COARSE, WIDE), BF16),
            vmem((REGIONS, CAP, BACK_CUT), BF16),
            vmem((REGIONS, CAP, WIDE - BACK_CUT), BF16),
            vmem((REGIONS, CAP, BACK_CUT), BF16),
            vmem((REGIONS, CAP, WIDE - BACK_CUT), BF16),
            vmem((2, FEAT, FINE), F32),
            vmem((8, COARSE), F32),
            vmem((SLOTS - 1, 8, COARSE), F32),
            vmem((8, COARSE), F32),
            vmem((REGIONS, 8, COARSE), F32),
            dma((3,)),
            dma((2, n)),
            dma((2, n)),
            dma((2, n)),
            dma((2, n)),
            dma((2, 3)),
            dma((2, 3)),
            dma((2, 2)),
            dma((2, 2)),
            dma((2, 3)),
            dma((2, 3)),
            dma((3,)),
            dma((3,)),
            dma((n,)),
            dma((n,)),
        ],
        compiler_params=pltpu.CompilerParams(
            collective_id=0, has_side_effects=True, vmem_limit_bytes=60 * 2**20
        ),
        name="hessian",
    )(
        owner_table.reshape(1, REGIONS * FINE),
        column_map.reshape(1, REGIONS * FINE),
        weight,
        vertical_modes.T,
        resid_part,
        perturb[0].transpose(1, 0, 2),
    )
    block = pl.BlockSpec((137, 2, FINE), lambda i: (i, 0, 0))
    product, next_residual = pl.pallas_call(
        last_step,
        grid=(FEAT // 137,),
        out_shape=(jax.ShapeDtypeStruct((FEAT, 2, FINE), F32),) * 2,
        in_specs=[
            block,
            block,
            pl.BlockSpec((1, FINE), lambda i: (0, 0)),
            pl.BlockSpec((8, COARSE), lambda i: (0, 0)),
        ],
        out_specs=(block, block),
        name="last_step",
    )(resid_part, increment, weight, step)
    return (product.transpose(1, 0, 2)[None], step[0:2, 0], next_residual.transpose(1, 0, 2)[None])


def solution(mesh):
    in_specs = (
        P("slot", None, None, "region"),
        P("slot", None, None, "region"),
        P(),
        P("region"),
        P(),
        P(),
    )
    out_specs = (P("slot", None, None, "region"), P(), P("slot", None, None, "region"))
    return jax.shard_map(
        per_device, mesh=mesh, in_specs=in_specs, out_specs=out_specs, check_vma=False
    )
```

```python
import jax
import jax.numpy as jnp
from jax import lax
from jax.experimental import pallas as pl
from jax.experimental.pallas import tpu as pltpu
from jax.sharding import PartitionSpec as P

MESH = pl.DeviceIdType.MESH
LAT_ROWS = 8
DIFFUSION_RATE = 0.2
F32 = jnp.float32
BF16 = jnp.bfloat16

REGIONS = 32
CAP = 32
SLOTS = 4
FINE = 512
COARSE = 128
FEAT = 685
FEAT_PAD = 704
WIDE = 1408
MEMBERS = 64
MODES = 10
ROWS = MODES * MEMBERS
SHARE = ROWS // SLOTS
OUT = ((0, 384, 0), (384, 384, 1), (768, 384, 0), (1152, 256, 1))
BACK = ((0, 384, 0), (384, 256, 1), (640, 384, 0), (1024, 384, 1))
LINE = ((2, 0), (2, 1), (1, 0), (3, 0), (1, 1), (3, 1), (0, 1))
GROUP = 8
GROUPS = MEMBERS // GROUP
SPREAD = MODES * GROUP
STEP = 176

NEAR_FIRST = (
    [(0, 1), (1, 0), (0, 3), (3, 0)],
    [(1, 1), (3, 3), (1, 3), (3, 1)],
    [(2, 0), (0, 2)],
    [(2, 1), (1, 2), (2, 3), (3, 2)],
    [(2, 2)],
)
HOPS = [(z, x, c) for group in NEAR_FIRST[::-1] for c in (0, 1) for z, x in group] + [(0, 0, 1)]


def smooth(cells, west_from, east_from):
    lane = lax.broadcasted_iota(jnp.int32, cells.shape, 1)
    row = lane % LAT_ROWS
    west = pltpu.roll(jnp.where(lane >= COARSE - LAT_ROWS, west_from, cells), LAT_ROWS, 1)
    east = pltpu.roll(jnp.where(lane < LAT_ROWS, east_from, cells), COARSE - LAT_ROWS, 1)
    south = pltpu.roll(cells, 1, 1)
    north = pltpu.roll(cells, COARSE - 1, 1)
    along = jnp.where(row > 0, south - cells, 0.0) + jnp.where(row < LAT_ROWS - 1, north - cells, 0.0)
    return cells + DIFFUSION_RATE * (west + east - 2.0 * cells + along)


def dot(a, b):
    return jnp.dot(a, b, preferred_element_type=F32)


def kernel(
    owners_ref,
    map_ref,
    weight_ref,
    modes_ref,
    resid_hbm,
    members_hbm,
    product_hbm,
    next_hbm,
    step_ref,
    resid,
    members,
    wide_rows,
    wide_cols,
    slot_hot_t,
    slot_hot,
    index_out,
    index_in,
    place,
    place_t,
    send,
    middle,
    part,
    part_in,
    coarse,
    modes_rep,
    mixer,
    mixer_t,
    gathered_modes,
    mode_cells,
    control,
    summed_in,
    edge_out,
    edge_in,
    shares,
    gathered,
    total,
    spread_out,
    spread_in,
    back,
    home,
    fine,
    stepped,
    norm,
    norm_in,
    norm_sum,
    norm_all,
    load_sem,
    index_send,
    index_recv,
    out_send,
    out_recv,
    part_send,
    part_recv,
    spread_send,
    spread_recv,
    back_send,
    back_recv,
    sum_send,
    sum_recv,
    edge_send,
    edge_recv,
    share_send,
    share_recv,
    norm_send,
    norm_recv,
    last_send,
    last_recv,
):
    me = lax.axis_index("region")
    slot = lax.axis_index("slot")
    z, x, core = me // 8, (me // 2) % 4, me % 2

    def region_at(hop):
        dz, dx, dc = hop
        return (((z + dz) % 4) * 4 + (x + dx) % 4) * 2 + (core + dc) % 2

    partners = [region_at(h) for h in HOPS]
    load_resid = [pltpu.make_async_copy(resid_hbm.at[:, v, :], resid.at[v], load_sem.at[v]) for v in range(2)]
    for copy in load_resid:
        copy.start()

    barrier = pltpu.get_barrier_semaphore()
    for p in partners:
        pl.semaphore_signal(barrier, inc=1, device_id={"region": p}, device_id_type=MESH)
    for d in (1, 2, 3):
        pl.semaphore_signal(barrier, inc=1, device_id={"slot": (slot + d) % SLOTS}, device_id_type=MESH)

    mine = pl.ds(pl.multiple_of(me * FINE, FINE), FINE)
    own = owners_ref[:, mine]
    owner_hot = (lax.broadcasted_iota(jnp.int32, (REGIONS, FINE), 0) == own).astype(BF16)
    earlier = (
        lax.broadcasted_iota(jnp.int32, (FINE, FINE), 0) < lax.broadcasted_iota(jnp.int32, (FINE, FINE), 1)
    ).astype(BF16)
    before = dot(owner_hot, earlier)
    rank = jnp.sum(owner_hot.astype(F32) * before, axis=0, keepdims=True)
    rank = rank.astype(jnp.int32)
    own_z, own_x, own_core = own // 8, (own // 2) % 4, own % 2
    index_row = (map_ref[:, mine] + 1).astype(F32)
    index_rows = jnp.broadcast_to(index_row, (16, FINE)).astype(BF16)
    for mode, (first, second) in enumerate(((own_z, own_x), (own_x, own_z))):
        my_slots = (first * 2 + own_core) * 128 + second * CAP + rank
        for q in range(4):
            hot = lax.broadcasted_iota(jnp.int32, (256, FINE), 0) + q * 256 == my_slots
            hot = hot.astype(F32).astype(BF16)
            slot_hot_t[mode, pl.ds(q * 256, 256), :] = hot
            got = lax.dot_general(
                index_rows, hot, (((1,), (1,)), ((), ())), preferred_element_type=F32
            ).astype(BF16)
            for e in range(2):
                index_out[mode, 2 * q + e] = got[:, e * 128 : (e + 1) * 128]

    spare = FEAT_PAD - FEAT
    wide_rows[pl.ds(FEAT, spare), :] = jnp.zeros((spare, FINE), F32)
    wide_rows[pl.ds(FEAT_PAD + FEAT, spare), :] = jnp.zeros((spare, FINE), F32)
    for v in range(2):
        load_resid[v].wait()
        wide_rows[pl.ds(v * FEAT_PAD, FEAT), :] = resid[v] * weight_ref[...]
    load_members = pltpu.make_async_copy(members_hbm, members.at[pl.ds(0, FEAT)], load_sem.at[2])
    load_members.start()
    for q in range(4):
        wide_cols[pl.ds(q * 128, 128), :] = wide_rows[:, q * 128 : (q + 1) * 128].T.astype(BF16)

    pl.semaphore_wait(barrier, len(HOPS) + 3)

    def spot(mode):
        return (z, x) if mode == 0 else (x, z)

    def device_at(mode, a, b, c):
        return ((a * 4 + b) if mode == 0 else (b * 4 + a)) * 2 + c

    def push(source, landing, send_sem, recv_sem, target):
        copy = pltpu.make_async_remote_copy(
            src_ref=source,
            dst_ref=landing,
            send_sem=send_sem,
            recv_sem=recv_sem,
            device_id=target,
            device_id_type=MESH,
        )
        copy.start()
        return copy

    def line_peers(mode):
        a, b = spot(mode)
        for j, (da, dc) in enumerate(LINE):
            a_to, c_to = (a + da) % 4, (core + dc) % 2
            yield j, a_to * 2 + c_to, {"region": device_at(mode, a_to, b, c_to)}

    def cross_peers(mode):
        a, b = spot(mode)
        for j, db in enumerate((2, 1, 3)):
            b_to = (b + db) % 4
            yield j, b_to, {"region": device_at(mode, a, b_to, core)}

    def pack(piece):
        left, width, mode = OUT[piece]

        def one(q, carry):
            rows = slot_hot_t[mode, pl.ds(pl.multiple_of(q * 256, 256), 256), :]
            got = dot(rows, wide_cols[:, left : left + width])
            send[piece][pl.ds(q * 2, 2)] = got.astype(BF16).reshape(2, 4, CAP, width)
            return carry

        lax.fori_loop(0, 4, one, 0)

    def out_start(piece, ahead):
        mode = OUT[piece][2]
        here = spot(mode)[0] * 2 + core
        copies = []
        for j, there, target in line_peers(mode):
            if ahead is not None:
                ahead[j].wait_send()
            copies.append(
                push(
                    send[piece].at[there],
                    middle[piece].at[:, here],
                    out_send.at[piece, j],
                    out_recv.at[piece, j],
                    target,
                )
            )
        middle[piece][:, here] = send[piece][here]
        return copies

    def part_start(piece):
        mode = OUT[piece][2]
        here = spot(mode)[1]
        for b in range(4):
            rows = middle[piece][b].reshape(8 * CAP, OUT[piece][1])
            part[piece][b] = dot(place_t[mode, b], rows).astype(BF16)
        copies = [
            push(
                part[piece].at[there],
                part_in[piece].at[here],
                part_send.at[piece, j],
                part_recv.at[piece, j],
                target,
            )
            for j, there, target in cross_peers(mode)
        ]
        part_in[piece][here] = part[piece][here]
        return copies

    def coarse_rows(piece):
        left, width, _ = OUT[piece]
        sums = part_in[piece][0].astype(F32)
        for b in range(1, 4):
            sums = sums + part_in[piece][b].astype(F32)
        coarse[pl.ds(left, width), :] = sums.T

    index_copies = []
    for mode in range(2):
        here = spot(mode)[0] * 2 + core
        for j, there, target in line_peers(mode):
            index_copies.append(
                push(
                    index_out.at[mode, there],
                    index_in.at[mode, here],
                    index_send.at[mode, j],
                    index_recv.at[mode, j],
                    target,
                )
            )
        index_in[mode, here] = index_out[mode, here]
    pack(0)
    out_0 = out_start(0, None)
    pack(1)
    out_1 = out_start(1, None)
    pack(2)
    pack(3)

    norm[...] = jnp.zeros_like(norm)
    for v in range(2):
        by_col = jnp.sum(resid[v] * resid[v], axis=0, keepdims=True)
        norm[pl.ds(v, 1), :] = by_col[:, 0:128] + by_col[:, 128:256] + by_col[:, 256:384] + by_col[:, 384:512]
    for mode in range(2):
        slot_hot[mode] = slot_hot_t[mode].T
    members[pl.ds(FEAT, spare)] = jnp.zeros((spare, MEMBERS, COARSE), BF16)

    repeat = (
        lax.broadcasted_iota(jnp.int32, (SPREAD, MODES), 0) // GROUP
        == lax.broadcasted_iota(jnp.int32, (SPREAD, MODES), 1)
    ).astype(F32).astype(BF16)
    high = modes_ref[...].astype(BF16)
    low = (modes_ref[...] - high.astype(F32)).astype(BF16)
    modes_rep[...] = jnp.zeros_like(modes_rep)
    modes_rep[pl.ds(0, FEAT), :] = jnp.concatenate([dot(repeat, high), dot(repeat, low)], axis=0).T

    def mixer_step(i, carry):
        cut = (32, GROUP, 2 * SPREAD)
        rows = modes_rep[pl.ds(pl.multiple_of(i * 32, 32), 32), :]
        same = lax.broadcasted_iota(jnp.int32, cut, 1) == lax.broadcasted_iota(jnp.int32, cut, 2) % GROUP
        block = jnp.where(same, jnp.broadcast_to(rows[:, None, :], cut), 0.0).reshape(256, 2 * SPREAD)
        at = pl.ds(pl.multiple_of(i * 256, 256), 256)
        mixer[at, :] = block.astype(BF16)
        mixer_t[:, at] = block.T.astype(BF16)
        return carry

    lax.fori_loop(0, FEAT_PAD // 32, mixer_step, 0)

    for copy in index_copies:
        copy.wait_recv()
    lane = lax.broadcasted_iota(jnp.int32, (8, COARSE), 1)
    for mode in range(2):
        tables = [index_in[mode, p].astype(F32)[0:8] for p in range(8)]
        for b in range(4):
            halves = []
            for h in range(2):
                row = jnp.zeros((8, COARSE), F32)
                for g in range(4):
                    shift = (g - b) * CAP % COARSE
                    table = tables[h * 4 + g]
                    row = jnp.where(lane // CAP == g, pltpu.roll(table, shift, 1) if shift else table, row)
                halves.append(row[0:1])
            row = jnp.concatenate(halves, axis=1)
            hot = (lax.broadcasted_iota(jnp.int32, (COARSE, 8 * CAP), 0) + 1).astype(F32) == row
            hot = hot.astype(F32)
            place_t[mode, b] = hot.astype(BF16)
            place[mode, b] = hot.T.astype(BF16)
    out_2 = out_start(2, out_0)
    out_3 = out_start(3, out_1)
    load_members.wait()

    def contract(v):
        gathered_modes[...] = jnp.zeros_like(gathered_modes)

        def chunk(i, carry):
            field = coarse[pl.ds(pl.multiple_of(v * FEAT_PAD + i * STEP, STEP), STEP), :]
            cells = members[pl.ds(i * STEP, STEP)].astype(F32).reshape(STEP, GROUPS, GROUP, COARSE)
            product = cells * field[:, None, None, :]
            left = mixer_t[:, pl.ds(pl.multiple_of(i * STEP * GROUP, STEP * GROUP), STEP * GROUP)]
            for pair in range(GROUPS // 2):
                both = jnp.concatenate(
                    [product[:, 2 * pair + e].reshape(STEP * GROUP, COARSE) for e in range(2)], axis=1
                )
                top = both.astype(BF16)
                rest = (both - top.astype(F32)).astype(BF16)
                main = dot(left, top)
                gathered_modes[:, pair * 256 : (pair + 1) * 256] += (
                    main[0:SPREAD] + main[SPREAD:] + dot(left[0:SPREAD], rest)
                )
            return carry

        lax.fori_loop(0, FEAT_PAD // STEP, chunk, 0)
        for m in range(MODES):
            for g in range(GROUPS):
                control[pl.ds(v * ROWS + m * MEMBERS + g * GROUP, GROUP), :] = gathered_modes[
                    m * GROUP : (m + 1) * GROUP, g * COARSE : (g + 1) * COARSE
                ]

    def share_rows(v, t):
        return pl.ds(pl.multiple_of(v * ROWS + t * SHARE, 8), SHARE)

    def sum_start(v):
        copies = []
        for d in (2, 1, 3):
            t = (slot + d) % SLOTS
            copy = pltpu.make_async_remote_copy(
                src_ref=control.at[share_rows(v, t)],
                dst_ref=summed_in.at[v, d - 1],
                send_sem=sum_send.at[v, d - 1],
                recv_sem=sum_recv.at[v, d - 1],
                device_id={"slot": t},
                device_id_type=MESH,
            )
            copy.start()
            copies.append(copy)
        return copies

    def edges_start(v):
        cells = control[share_rows(v, slot), :]
        for d in range(3):
            cells = cells + summed_in[v, d]
        shares[v] = cells
        lane = lax.broadcasted_iota(jnp.int32, (40, COARSE), 1)
        east = jnp.zeros((40, COARSE), F32)
        west = jnp.zeros((40, COARSE), F32)
        for g in range(4):
            part = cells[g * 40 : (g + 1) * 40]
            mine = lane // 16 == g
            east = jnp.where(mine, pltpu.roll(part, 16 * g + 16, 1), east)
            west = jnp.where(mine, pltpu.roll(part, 16 * g, 1) if g else part, west)
        edge_out[v, 0] = east
        edge_out[v, 1] = west
        copies = []
        for side, p in ((0, (me + 1) % REGIONS), (1, (me + REGIONS - 1) % REGIONS)):
            copy = pltpu.make_async_remote_copy(
                src_ref=edge_out.at[v, side],
                dst_ref=edge_in.at[v, side],
                send_sem=edge_send.at[v, side],
                recv_sem=edge_recv.at[v, side],
                device_id={"region": p},
                device_id_type=MESH,
            )
            copy.start()
            copies.append(copy)
        return copies

    def smooth_share(v):
        cells = shares[v]
        lane = lax.broadcasted_iota(jnp.int32, (SHARE, COARSE), 1)
        west = jnp.concatenate([pltpu.roll(edge_in[v, 0], 112 - 16 * g, 1) for g in range(4)], axis=0)
        east = jnp.concatenate(
            [pltpu.roll(edge_in[v, 1], 128 - 16 * g, 1) if g else edge_in[v, 1] for g in range(4)], axis=0
        )
        once = smooth(cells, west, east)
        west = jnp.where(lane < LAT_ROWS, cells, west)
        east = jnp.where(lane >= COARSE - LAT_ROWS, cells, east)
        twice = smooth(once, smooth(west, west, west), smooth(east, east, east))
        norm[pl.ds(2 + v, 1), :] = jnp.sum(once * once, axis=0, keepdims=True)
        smooth_bits = twice.astype(BF16)
        gathered[v, slot] = smooth_bits
        copies = []
        for d in (2, 1, 3):
            copy = pltpu.make_async_remote_copy(
                src_ref=gathered.at[v, slot],
                dst_ref=gathered.at[v, slot],
                send_sem=share_send.at[v, d - 1],
                recv_sem=share_recv.at[v, d - 1],
                device_id={"slot": (slot + d) % SLOTS},
                device_id_type=MESH,
            )
            copy.start()
            copies.append(copy)
        return copies

    def expand(v):
        every = jnp.concatenate([gathered[v, t].astype(F32) for t in range(SLOTS)], axis=0)
        for g in range(GROUPS):
            cells = jnp.concatenate(
                [every[m * MEMBERS + g * GROUP : m * MEMBERS + (g + 1) * GROUP] for m in range(MODES)], axis=0
            ).astype(BF16)
            mode_cells[0:SPREAD, g * COARSE : (g + 1) * COARSE] = cells
            mode_cells[SPREAD:, g * COARSE : (g + 1) * COARSE] = cells

        def chunk(i, carry):
            left = mixer[pl.ds(pl.multiple_of(i * STEP * GROUP, STEP * GROUP), STEP * GROUP), :]
            cells = members[pl.ds(i * STEP, STEP)].astype(F32).reshape(STEP, GROUPS, GROUP, COARSE)
            sums = jnp.zeros((STEP, GROUP, COARSE), F32)
            for pair in range(GROUPS // 2):
                mixed = dot(left, mode_cells[:, pair * 256 : (pair + 1) * 256])
                for e in range(2):
                    part = mixed[:, e * COARSE : (e + 1) * COARSE].reshape(STEP, GROUP, COARSE)
                    sums = sums + cells[:, 2 * pair + e] * part
            at = pl.ds(pl.multiple_of(v * FEAT_PAD + i * STEP, STEP), STEP)
            total[at, :] = jnp.sum(sums, axis=1)
            return carry

        lax.fori_loop(0, FEAT_PAD // STEP, chunk, 0)

    def arrived(copies):
        for copy in copies:
            copy.wait_recv()

    def spread_start(piece):
        left, width, mode = BACK[piece]
        here = spot(mode)[1]
        spread_out[piece][...] = total[pl.ds(left, width), :].T.astype(BF16)
        copies = [
            push(
                spread_out[piece],
                spread_in[piece].at[here],
                spread_send.at[piece, j],
                spread_recv.at[piece, j],
                target,
            )
            for j, _, target in cross_peers(mode)
        ]
        spread_in[piece][here] = spread_out[piece][...]
        return copies

    def back_start(piece):
        _, width, mode = BACK[piece]
        here = spot(mode)[0] * 2 + core
        for b in range(4):
            rows = dot(place[mode, b], spread_in[piece][b])
            back[piece][:, b] = rows.astype(BF16).reshape(8, CAP, width)
        copies = [
            push(
                back[piece].at[there],
                home[piece].at[here],
                back_send.at[piece, j],
                back_recv.at[piece, j],
                target,
            )
            for j, there, target in line_peers(mode)
        ]
        home[piece][here] = back[piece][here]
        return copies

    def fine_rows(piece):
        left, width, mode = BACK[piece]
        source = home[piece][...].reshape(REGIONS * CAP, width)
        for q in range(4):
            cols = slice(q * 128, (q + 1) * 128)
            rows = dot(slot_hot[mode, pl.ds(q * 128, 128), :], source).T
            for v in range(2):
                first = max(left, v * FEAT_PAD)
                last = min(left + width, v * FEAT_PAD + FEAT)
                if first < last:
                    fine[v, first - v * FEAT_PAD : last - v * FEAT_PAD, cols] = rows[first - left : last - left]

    def store_start(v, step):
        product = resid[v] + fine[v] * weight_ref[...]
        fine[v] = product
        stepped[v] = resid[v] - step[v : v + 1, 0:1] * product
        copies = [
            pltpu.make_async_copy(fine.at[v], product_hbm.at[:, v, :], load_sem.at[v]),
            pltpu.make_async_copy(stepped.at[v], next_hbm.at[:, v, :], load_sem.at[3 + v]),
        ]
        for copy in copies:
            copy.start()
        return copies

    arrived(out_0)
    part_0 = part_start(0)
    arrived(out_1)
    part_1 = part_start(1)
    total[pl.ds(FEAT_PAD, FEAT_PAD), :] = jnp.zeros((FEAT_PAD, COARSE), F32)
    arrived(part_0)
    coarse_rows(0)
    arrived(part_1)
    coarse_rows(1)
    contract(0)
    sum_copies = sum_start(0)
    arrived(out_2)
    part_2 = part_start(2)
    arrived(out_3)
    part_3 = part_start(3)
    arrived(sum_copies)
    edge_copies = edges_start(0)
    arrived(edge_copies)
    share_copies = smooth_share(0)

    arrived(part_2)
    coarse_rows(2)
    arrived(part_3)
    coarse_rows(3)
    contract(1)
    sum_copies_b = sum_start(1)

    arrived(share_copies)
    expand(0)
    spread_0 = spread_start(0)
    spread_1 = spread_start(1)
    arrived(sum_copies_b)
    edge_copies_b = edges_start(1)
    arrived(spread_0)
    back_0 = back_start(0)
    arrived(spread_1)
    back_1 = back_start(1)
    arrived(edge_copies_b)
    share_copies_b = smooth_share(1)
    norm_copies = []
    for d in (2, 1, 3):
        copy = pltpu.make_async_remote_copy(
            src_ref=norm,
            dst_ref=norm_in.at[d - 1],
            send_sem=norm_send.at[d - 1],
            recv_sem=norm_recv.at[d - 1],
            device_id={"slot": (slot + d) % SLOTS},
            device_id_type=MESH,
        )
        copy.start()
        norm_copies.append(copy)
    arrived(share_copies_b)
    expand(1)
    spread_2 = spread_start(2)
    spread_3 = spread_start(3)
    arrived(norm_copies)
    norm_sum[...] = norm[...] + norm_in[0] + norm_in[1] + norm_in[2]
    last_copies = []
    for i, p in enumerate(partners):
        copy = pltpu.make_async_remote_copy(
            src_ref=norm_sum,
            dst_ref=norm_all.at[me],
            send_sem=last_send.at[i],
            recv_sem=last_recv.at[i],
            device_id={"region": p},
            device_id_type=MESH,
        )
        copy.start()
        last_copies.append(copy)
    norm_all[me] = norm_sum[...]

    arrived(spread_2)
    back_2 = back_start(2)
    arrived(spread_3)
    back_3 = back_start(3)

    arrived(back_0)
    fine_rows(0)
    arrived(back_1)
    fine_rows(1)
    arrived(last_copies)
    sums = jnp.sum(jnp.sum(norm_all[...], axis=0), axis=1, keepdims=True)
    squares = jnp.broadcast_to(sums, (8, COARSE))
    step = squares / (squares + pltpu.roll(squares, 6, 0))
    step_ref[...] = step
    arrived(back_2)
    fine_rows(2)
    stores = store_start(0, step)
    arrived(back_3)
    fine_rows(3)
    stores += store_start(1, step)
    for copies in (
        index_copies,
        out_2,
        out_3,
        part_0,
        part_1,
        part_2,
        part_3,
        sum_copies,
        sum_copies_b,
        edge_copies,
        edge_copies_b,
        share_copies,
        share_copies_b,
        norm_copies,
        last_copies,
        spread_0,
        spread_1,
        spread_2,
        spread_3,
        back_0,
        back_1,
        back_2,
        back_3,
    ):
        for copy in copies:
            copy.wait_send()
    for copy in stores:
        copy.wait()


def per_device(residual, perturb, vertical_modes, column_weight, owner_table, column_map):
    vmem, dma = pltpu.VMEM, pltpu.SemaphoreType.DMA
    resid_part = residual[0].transpose(1, 0, 2)
    weight = column_weight.reshape(1, FINE)
    whole = pl.BlockSpec(memory_space=pltpu.VMEM)
    anywhere = pl.BlockSpec(memory_space=pl.ANY)
    n = len(HOPS)
    product, next_residual, step = pl.pallas_call(
        kernel,
        out_shape=(
            jax.ShapeDtypeStruct((FEAT, 2, FINE), F32),
            jax.ShapeDtypeStruct((FEAT, 2, FINE), F32),
            jax.ShapeDtypeStruct((8, COARSE), F32),
        ),
        in_specs=[whole] * 4 + [anywhere] * 2,
        out_specs=(anywhere, anywhere, whole),
        scratch_shapes=[
            vmem((2, FEAT, FINE), F32),
            vmem((FEAT_PAD, MEMBERS, COARSE), BF16),
            vmem((WIDE, FINE), F32),
            vmem((FINE, WIDE), BF16),
            vmem((2, REGIONS * CAP, FINE), BF16),
            vmem((2, FINE, REGIONS * CAP), BF16),
            vmem((2, 8, 16, COARSE), BF16),
            vmem((2, 8, 16, COARSE), BF16),
            vmem((2, 4, 8 * CAP, COARSE), BF16),
            vmem((2, 4, COARSE, 8 * CAP), BF16),
            [vmem((8, 4, CAP, width), BF16) for _, width, _ in OUT],
            [vmem((4, 8, CAP, width), BF16) for _, width, _ in OUT],
            [vmem((4, COARSE, width), BF16) for _, width, _ in OUT],
            [vmem((4, COARSE, width), BF16) for _, width, _ in OUT],
            vmem((WIDE, COARSE), F32),
            vmem((FEAT_PAD, 2 * SPREAD), F32),
            vmem((FEAT_PAD * GROUP, 2 * SPREAD), BF16),
            vmem((2 * SPREAD, FEAT_PAD * GROUP), BF16),
            vmem((SPREAD, GROUPS * COARSE), F32),
            vmem((2 * SPREAD, GROUPS * COARSE), BF16),
            vmem((2 * ROWS, COARSE), F32),
            vmem((2, SLOTS - 1, SHARE, COARSE), F32),
            vmem((2, 2, 40, COARSE), F32),
            vmem((2, 2, 40, COARSE), F32),
            vmem((2, SHARE, COARSE), F32),
            vmem((2, SLOTS, SHARE, COARSE), BF16),
            vmem((WIDE, COARSE), F32),
            [vmem((COARSE, width), BF16) for _, width, _ in BACK],
            [vmem((4, COARSE, width), BF16) for _, width, _ in BACK],
            [vmem((8, 4, CAP, width), BF16) for _, width, _ in BACK],
            [vmem((8, 4, CAP, width), BF16) for _, width, _ in BACK],
            vmem((2, FEAT, FINE), F32),
            vmem((2, FEAT, FINE), F32),
            vmem((8, COARSE), F32),
            vmem((SLOTS - 1, 8, COARSE), F32),
            vmem((8, COARSE), F32),
            vmem((REGIONS, 8, COARSE), F32),
            dma((5,)),
            *[dma((rows, cols)) for rows, cols in ((2, 7), (4, 7), (4, 3), (4, 3), (4, 7)) for _ in range(2)],
            dma((2, 3)),
            dma((2, 3)),
            dma((2, 2)),
            dma((2, 2)),
            dma((2, 3)),
            dma((2, 3)),
            dma((3,)),
            dma((3,)),
            dma((n,)),
            dma((n,)),
        ],
        compiler_params=pltpu.CompilerParams(
            collective_id=0, has_side_effects=True, vmem_limit_bytes=60 * 2**20
        ),
        name="hessian",
    )(
        owner_table.reshape(1, REGIONS * FINE),
        column_map.reshape(1, REGIONS * FINE),
        weight,
        vertical_modes.T,
        resid_part,
        perturb[0].transpose(1, 0, 2),
    )
    return (product.transpose(1, 0, 2)[None], step[0:2, 0], next_residual.transpose(1, 0, 2)[None])


def solution(mesh):
    in_specs = (
        P("slot", None, None, "region"),
        P("slot", None, None, "region"),
        P(),
        P("region"),
        P(),
        P(),
    )
    out_specs = (P("slot", None, None, "region"), P(), P("slot", None, None, "region"))
    return jax.shard_map(
        per_device, mesh=mesh, in_specs=in_specs, out_specs=out_specs, check_vma=False
    )
```

```python
import jax
import jax.numpy as jnp
from jax import lax
from jax.experimental import pallas as pl
from jax.experimental.pallas import tpu as pltpu
from jax.sharding import PartitionSpec as P

MESH = pl.DeviceIdType.MESH
LAT_ROWS = 8
DIFFUSION_RATE = 0.2
F32 = jnp.float32
BF16 = jnp.bfloat16

REGIONS = 32
CAP = 32
SLOTS = 4
FINE = 512
COARSE = 128
FEAT = 685
FEAT_PAD = 704
WIDE = 1408
MEMBERS = 64
MODES = 10
ROWS = MODES * MEMBERS
SHARE = ROWS // SLOTS
OUT = ((0, 384, 0), (384, 384, 1), (768, 384, 0), (1152, 256, 1))
BACK = ((0, 384, 0), (384, 256, 1), (640, 256, 0), (896, 256, 1), (1152, 128, 0), (1280, 128, 1))
LINE = ((2, 0), (2, 1), (1, 0), (3, 0), (1, 1), (3, 1), (0, 1))
GROUP = 8
GROUPS = MEMBERS // GROUP
SPREAD = MODES * GROUP
STEP = 176

NEAR_FIRST = (
    [(0, 1), (1, 0), (0, 3), (3, 0)],
    [(1, 1), (3, 3), (1, 3), (3, 1)],
    [(2, 0), (0, 2)],
    [(2, 1), (1, 2), (2, 3), (3, 2)],
    [(2, 2)],
)
HOPS = [(z, x, c) for group in NEAR_FIRST[::-1] for c in (0, 1) for z, x in group] + [(0, 0, 1)]


def smooth(cells, west_from, east_from):
    lane = lax.broadcasted_iota(jnp.int32, cells.shape, 1)
    row = lane % LAT_ROWS
    west = pltpu.roll(jnp.where(lane >= COARSE - LAT_ROWS, west_from, cells), LAT_ROWS, 1)
    east = pltpu.roll(jnp.where(lane < LAT_ROWS, east_from, cells), COARSE - LAT_ROWS, 1)
    south = pltpu.roll(cells, 1, 1)
    north = pltpu.roll(cells, COARSE - 1, 1)
    along = jnp.where(row > 0, south - cells, 0.0) + jnp.where(row < LAT_ROWS - 1, north - cells, 0.0)
    return cells + DIFFUSION_RATE * (west + east - 2.0 * cells + along)


def dot(a, b):
    return jnp.dot(a, b, preferred_element_type=F32)


def kernel(
    owners_ref,
    map_ref,
    weight_ref,
    modes_ref,
    resid_hbm,
    members_hbm,
    fine_hbm,
    step_ref,
    resid,
    members,
    wide_rows,
    wide_cols,
    slot_hot_t,
    slot_hot,
    index_out,
    index_in,
    place,
    place_t,
    send,
    middle,
    part,
    part_in,
    coarse,
    modes_rep,
    mixer,
    mixer_t,
    gathered_modes,
    mode_cells,
    control,
    summed_in,
    edge_out,
    edge_in,
    shares,
    gathered,
    total,
    spread_out,
    spread_in,
    back,
    home,
    fine,
    norm,
    norm_in,
    norm_sum,
    norm_all,
    load_sem,
    index_send,
    index_recv,
    out_send,
    out_recv,
    part_send,
    part_recv,
    spread_send,
    spread_recv,
    back_send,
    back_recv,
    sum_send,
    sum_recv,
    edge_send,
    edge_recv,
    share_send,
    share_recv,
    norm_send,
    norm_recv,
    last_send,
    last_recv,
):
    me = lax.axis_index("region")
    slot = lax.axis_index("slot")
    z, x, core = me // 8, (me // 2) % 4, me % 2

    def region_at(hop):
        dz, dx, dc = hop
        return (((z + dz) % 4) * 4 + (x + dx) % 4) * 2 + (core + dc) % 2

    partners = [region_at(h) for h in HOPS]
    load_resid = [pltpu.make_async_copy(resid_hbm.at[:, v, :], resid.at[v], load_sem.at[v]) for v in range(2)]
    for copy in load_resid:
        copy.start()

    barrier = pltpu.get_barrier_semaphore()
    for p in partners:
        pl.semaphore_signal(barrier, inc=1, device_id={"region": p}, device_id_type=MESH)
    for d in (1, 2, 3):
        pl.semaphore_signal(barrier, inc=1, device_id={"slot": (slot + d) % SLOTS}, device_id_type=MESH)

    mine = pl.ds(pl.multiple_of(me * FINE, FINE), FINE)
    own = owners_ref[:, mine]
    owner_hot = (lax.broadcasted_iota(jnp.int32, (REGIONS, FINE), 0) == own).astype(BF16)
    earlier = (
        lax.broadcasted_iota(jnp.int32, (FINE, FINE), 0) < lax.broadcasted_iota(jnp.int32, (FINE, FINE), 1)
    ).astype(BF16)
    before = dot(owner_hot, earlier)
    rank = jnp.sum(owner_hot.astype(F32) * before, axis=0, keepdims=True)
    rank = rank.astype(jnp.int32)
    own_z, own_x, own_core = own // 8, (own // 2) % 4, own % 2
    index_row = (map_ref[:, mine] + 1).astype(F32)
    index_rows = jnp.broadcast_to(index_row, (16, FINE)).astype(BF16)
    for mode, (first, second) in enumerate(((own_z, own_x), (own_x, own_z))):
        my_slots = (first * 2 + own_core) * 128 + second * CAP + rank
        for q in range(4):
            hot = lax.broadcasted_iota(jnp.int32, (256, FINE), 0) + q * 256 == my_slots
            hot = hot.astype(F32).astype(BF16)
            slot_hot_t[mode, pl.ds(q * 256, 256), :] = hot
            got = lax.dot_general(
                index_rows, hot, (((1,), (1,)), ((), ())), preferred_element_type=F32
            ).astype(BF16)
            for e in range(2):
                index_out[mode, 2 * q + e] = got[:, e * 128 : (e + 1) * 128]

    spare = FEAT_PAD - FEAT
    wide_rows[pl.ds(FEAT, spare), :] = jnp.zeros((spare, FINE), F32)
    wide_rows[pl.ds(FEAT_PAD + FEAT, spare), :] = jnp.zeros((spare, FINE), F32)
    pl.semaphore_wait(barrier, len(HOPS) + 3)

    def spot(mode):
        return (z, x) if mode == 0 else (x, z)

    def device_at(mode, a, b, c):
        return ((a * 4 + b) if mode == 0 else (b * 4 + a)) * 2 + c

    def push(source, landing, send_sem, recv_sem, target):
        copy = pltpu.make_async_remote_copy(
            src_ref=source,
            dst_ref=landing,
            send_sem=send_sem,
            recv_sem=recv_sem,
            device_id=target,
            device_id_type=MESH,
        )
        copy.start()
        return copy

    def line_peers(mode):
        a, b = spot(mode)
        for j, (da, dc) in enumerate(LINE):
            a_to, c_to = (a + da) % 4, (core + dc) % 2
            yield j, a_to * 2 + c_to, {"region": device_at(mode, a_to, b, c_to)}

    def cross_peers(mode):
        a, b = spot(mode)
        for j, db in enumerate((2, 1, 3)):
            b_to = (b + db) % 4
            yield j, b_to, {"region": device_at(mode, a, b_to, core)}

    def weigh(v):
        load_resid[v].wait()
        wide_rows[pl.ds(v * FEAT_PAD, FEAT), :] = resid[v] * weight_ref[...]

    def pack(piece):
        left, width, mode = OUT[piece]
        for q in range(4):
            cols = slice(q * 128, (q + 1) * 128)
            wide_cols[cols, left : left + width] = wide_rows[left : left + width, cols].T.astype(BF16)

        def one(q, carry):
            rows = slot_hot_t[mode, pl.ds(pl.multiple_of(q * 256, 256), 256), :]
            got = dot(rows, wide_cols[:, left : left + width])
            send[piece][pl.ds(q * 2, 2)] = got.astype(BF16).reshape(2, 4, CAP, width)
            return carry

        lax.fori_loop(0, 4, one, 0)

    def out_start(piece, ahead):
        mode = OUT[piece][2]
        here = spot(mode)[0] * 2 + core
        copies = []
        for j, there, target in line_peers(mode):
            if ahead is not None:
                ahead[j].wait_send()
            copies.append(
                push(
                    send[piece].at[there],
                    middle[piece].at[:, here],
                    out_send.at[piece, j],
                    out_recv.at[piece, j],
                    target,
                )
            )
        middle[piece][:, here] = send[piece][here]
        return copies

    def part_start(piece):
        mode = OUT[piece][2]
        here = spot(mode)[1]
        for b in range(4):
            rows = middle[piece][b].reshape(8 * CAP, OUT[piece][1])
            part[piece][b] = dot(place_t[mode, b], rows).astype(BF16)
        copies = [
            push(
                part[piece].at[there],
                part_in[piece].at[here],
                part_send.at[piece, j],
                part_recv.at[piece, j],
                target,
            )
            for j, there, target in cross_peers(mode)
        ]
        part_in[piece][here] = part[piece][here]
        return copies

    def coarse_rows(piece):
        left, width, _ = OUT[piece]
        sums = part_in[piece][0].astype(F32)
        for b in range(1, 4):
            sums = sums + part_in[piece][b].astype(F32)
        coarse[pl.ds(left, width), :] = sums.T

    index_copies = []
    for mode in range(2):
        here = spot(mode)[0] * 2 + core
        for j, there, target in line_peers(mode):
            index_copies.append(
                push(
                    index_out.at[mode, there],
                    index_in.at[mode, here],
                    index_send.at[mode, j],
                    index_recv.at[mode, j],
                    target,
                )
            )
        index_in[mode, here] = index_out[mode, here]
    weigh(0)
    pack(0)
    out_0 = out_start(0, None)
    weigh(1)
    load_members = pltpu.make_async_copy(members_hbm, members.at[pl.ds(0, FEAT)], load_sem.at[2])
    load_members.start()
    pack(1)
    out_1 = out_start(1, None)
    pack(2)
    pack(3)

    norm[...] = jnp.zeros_like(norm)
    for v in range(2):
        by_col = jnp.sum(resid[v] * resid[v], axis=0, keepdims=True)
        norm[pl.ds(v, 1), :] = by_col[:, 0:128] + by_col[:, 128:256] + by_col[:, 256:384] + by_col[:, 384:512]
    for mode in range(2):
        slot_hot[mode] = slot_hot_t[mode].T
    members[pl.ds(FEAT, spare)] = jnp.zeros((spare, MEMBERS, COARSE), BF16)

    repeat = (
        lax.broadcasted_iota(jnp.int32, (SPREAD, MODES), 0) // GROUP
        == lax.broadcasted_iota(jnp.int32, (SPREAD, MODES), 1)
    ).astype(F32).astype(BF16)
    high = modes_ref[...].astype(BF16)
    low = (modes_ref[...] - high.astype(F32)).astype(BF16)
    modes_rep[...] = jnp.zeros_like(modes_rep)
    modes_rep[pl.ds(0, FEAT), :] = jnp.concatenate([dot(repeat, high), dot(repeat, low)], axis=0).T

    def mixer_step(i, carry):
        cut = (32, GROUP, 2 * SPREAD)
        rows = modes_rep[pl.ds(pl.multiple_of(i * 32, 32), 32), :]
        same = lax.broadcasted_iota(jnp.int32, cut, 1) == lax.broadcasted_iota(jnp.int32, cut, 2) % GROUP
        block = jnp.where(same, jnp.broadcast_to(rows[:, None, :], cut), 0.0).reshape(256, 2 * SPREAD)
        at = pl.ds(pl.multiple_of(i * 256, 256), 256)
        mixer[at, :] = block.astype(BF16)
        mixer_t[:, at] = block.T.astype(BF16)
        return carry

    lax.fori_loop(0, FEAT_PAD // 32, mixer_step, 0)

    for copy in index_copies:
        copy.wait_recv()
    lane = lax.broadcasted_iota(jnp.int32, (8, COARSE), 1)
    for mode in range(2):
        tables = [index_in[mode, p].astype(F32)[0:8] for p in range(8)]
        for b in range(4):
            halves = []
            for h in range(2):
                row = jnp.zeros((8, COARSE), F32)
                for g in range(4):
                    shift = (g - b) * CAP % COARSE
                    table = tables[h * 4 + g]
                    row = jnp.where(lane // CAP == g, pltpu.roll(table, shift, 1) if shift else table, row)
                halves.append(row[0:1])
            row = jnp.concatenate(halves, axis=1)
            hot = (lax.broadcasted_iota(jnp.int32, (COARSE, 8 * CAP), 0) + 1).astype(F32) == row
            hot = hot.astype(F32)
            place_t[mode, b] = hot.astype(BF16)
            place[mode, b] = hot.T.astype(BF16)
    load_members.wait()

    def contract(v):
        gathered_modes[...] = jnp.zeros_like(gathered_modes)

        def chunk(i, carry):
            field = coarse[pl.ds(pl.multiple_of(v * FEAT_PAD + i * STEP, STEP), STEP), :]
            cells = members[pl.ds(i * STEP, STEP)].astype(F32).reshape(STEP, GROUPS, GROUP, COARSE)
            product = cells * field[:, None, None, :]
            left = mixer_t[:, pl.ds(pl.multiple_of(i * STEP * GROUP, STEP * GROUP), STEP * GROUP)]
            for pair in range(GROUPS // 2):
                both = jnp.concatenate(
                    [product[:, 2 * pair + e].reshape(STEP * GROUP, COARSE) for e in range(2)], axis=1
                )
                top = both.astype(BF16)
                rest = (both - top.astype(F32)).astype(BF16)
                main = dot(left, top)
                gathered_modes[:, pair * 256 : (pair + 1) * 256] += (
                    main[0:SPREAD] + main[SPREAD:] + dot(left[0:SPREAD], rest)
                )
            return carry

        lax.fori_loop(0, FEAT_PAD // STEP, chunk, 0)
        for m in range(MODES):
            for g in range(GROUPS):
                control[pl.ds(v * ROWS + m * MEMBERS + g * GROUP, GROUP), :] = gathered_modes[
                    m * GROUP : (m + 1) * GROUP, g * COARSE : (g + 1) * COARSE
                ]

    def share_rows(v, t):
        return pl.ds(pl.multiple_of(v * ROWS + t * SHARE, 8), SHARE)

    def sum_start(v):
        copies = []
        for d in (2, 1, 3):
            t = (slot + d) % SLOTS
            copy = pltpu.make_async_remote_copy(
                src_ref=control.at[share_rows(v, t)],
                dst_ref=summed_in.at[v, d - 1],
                send_sem=sum_send.at[v, d - 1],
                recv_sem=sum_recv.at[v, d - 1],
                device_id={"slot": t},
                device_id_type=MESH,
            )
            copy.start()
            copies.append(copy)
        return copies

    def edges_start(v):
        cells = control[share_rows(v, slot), :]
        for d in range(3):
            cells = cells + summed_in[v, d]
        shares[v] = cells
        lane = lax.broadcasted_iota(jnp.int32, (40, COARSE), 1)
        east = jnp.zeros((40, COARSE), F32)
        west = jnp.zeros((40, COARSE), F32)
        for g in range(4):
            part = cells[g * 40 : (g + 1) * 40]
            mine = lane // 16 == g
            east = jnp.where(mine, pltpu.roll(part, 16 * g + 16, 1), east)
            west = jnp.where(mine, pltpu.roll(part, 16 * g, 1) if g else part, west)
        edge_out[v, 0] = east
        edge_out[v, 1] = west
        copies = []
        for side, p in ((0, (me + 1) % REGIONS), (1, (me + REGIONS - 1) % REGIONS)):
            copy = pltpu.make_async_remote_copy(
                src_ref=edge_out.at[v, side],
                dst_ref=edge_in.at[v, side],
                send_sem=edge_send.at[v, side],
                recv_sem=edge_recv.at[v, side],
                device_id={"region": p},
                device_id_type=MESH,
            )
            copy.start()
            copies.append(copy)
        return copies

    def smooth_share(v):
        cells = shares[v]
        lane = lax.broadcasted_iota(jnp.int32, (SHARE, COARSE), 1)
        west = jnp.concatenate([pltpu.roll(edge_in[v, 0], 112 - 16 * g, 1) for g in range(4)], axis=0)
        east = jnp.concatenate(
            [pltpu.roll(edge_in[v, 1], 128 - 16 * g, 1) if g else edge_in[v, 1] for g in range(4)], axis=0
        )
        once = smooth(cells, west, east)
        west = jnp.where(lane < LAT_ROWS, cells, west)
        east = jnp.where(lane >= COARSE - LAT_ROWS, cells, east)
        twice = smooth(once, smooth(west, west, west), smooth(east, east, east))
        norm[pl.ds(2 + v, 1), :] = jnp.sum(once * once, axis=0, keepdims=True)
        smooth_bits = twice.astype(BF16)
        gathered[v, slot] = smooth_bits
        copies = []
        for d in (2, 1, 3):
            copy = pltpu.make_async_remote_copy(
                src_ref=gathered.at[v, slot],
                dst_ref=gathered.at[v, slot],
                send_sem=share_send.at[v, d - 1],
                recv_sem=share_recv.at[v, d - 1],
                device_id={"slot": (slot + d) % SLOTS},
                device_id_type=MESH,
            )
            copy.start()
            copies.append(copy)
        return copies

    def expand(v):
        every = jnp.concatenate([gathered[v, t].astype(F32) for t in range(SLOTS)], axis=0)
        for g in range(GROUPS):
            cells = jnp.concatenate(
                [every[m * MEMBERS + g * GROUP : m * MEMBERS + (g + 1) * GROUP] for m in range(MODES)], axis=0
            ).astype(BF16)
            mode_cells[0:SPREAD, g * COARSE : (g + 1) * COARSE] = cells
            mode_cells[SPREAD:, g * COARSE : (g + 1) * COARSE] = cells

        def chunk(i, carry):
            left = mixer[pl.ds(pl.multiple_of(i * STEP * GROUP, STEP * GROUP), STEP * GROUP), :]
            cells = members[pl.ds(i * STEP, STEP)].astype(F32).reshape(STEP, GROUPS, GROUP, COARSE)
            sums = jnp.zeros((STEP, GROUP, COARSE), F32)
            for pair in range(GROUPS // 2):
                mixed = dot(left, mode_cells[:, pair * 256 : (pair + 1) * 256])
                for e in range(2):
                    part = mixed[:, e * COARSE : (e + 1) * COARSE].reshape(STEP, GROUP, COARSE)
                    sums = sums + cells[:, 2 * pair + e] * part
            at = pl.ds(pl.multiple_of(v * FEAT_PAD + i * STEP, STEP), STEP)
            total[at, :] = jnp.sum(sums, axis=1)
            return carry

        lax.fori_loop(0, FEAT_PAD // STEP, chunk, 0)

    def arrived(copies):
        for copy in copies:
            copy.wait_recv()

    def spread_start(piece):
        left, width, mode = BACK[piece]
        here = spot(mode)[1]
        spread_out[piece][...] = total[pl.ds(left, width), :].T.astype(BF16)
        copies = [
            push(
                spread_out[piece],
                spread_in[piece].at[here],
                spread_send.at[piece, j],
                spread_recv.at[piece, j],
                target,
            )
            for j, _, target in cross_peers(mode)
        ]
        spread_in[piece][here] = spread_out[piece][...]
        return copies

    def back_start(piece):
        _, width, mode = BACK[piece]
        here = spot(mode)[0] * 2 + core
        for b in range(4):
            rows = dot(place[mode, b], spread_in[piece][b])
            back[piece][:, b] = rows.astype(BF16).reshape(8, CAP, width)
        copies = [
            push(
                back[piece].at[there],
                home[piece].at[here],
                back_send.at[piece, j],
                back_recv.at[piece, j],
                target,
            )
            for j, there, target in line_peers(mode)
        ]
        home[piece][here] = back[piece][here]
        return copies

    def fine_rows(piece):
        left, width, mode = BACK[piece]
        source = home[piece][...].reshape(REGIONS * CAP, width)
        for q in range(4):
            cols = slice(q * 128, (q + 1) * 128)
            rows = dot(slot_hot[mode, pl.ds(q * 128, 128), :], source).T
            for v in range(2):
                first = max(left, v * FEAT_PAD)
                last = min(left + width, v * FEAT_PAD + FEAT)
                if first < last:
                    fine[v, first - v * FEAT_PAD : last - v * FEAT_PAD, cols] = rows[first - left : last - left]

    def store_start(v):
        copies = [pltpu.make_async_copy(fine.at[v], fine_hbm.at[:, v, :], load_sem.at[v])]
        for copy in copies:
            copy.start()
        return copies

    arrived(out_0)
    part_0 = part_start(0)
    arrived(out_1)
    part_1 = part_start(1)
    out_2 = out_start(2, out_0)
    out_3 = out_start(3, out_1)
    total[pl.ds(FEAT_PAD, FEAT_PAD), :] = jnp.zeros((FEAT_PAD, COARSE), F32)
    arrived(part_0)
    coarse_rows(0)
    arrived(part_1)
    coarse_rows(1)
    contract(0)
    sum_copies = sum_start(0)
    arrived(out_2)
    part_2 = part_start(2)
    arrived(out_3)
    part_3 = part_start(3)
    arrived(sum_copies)
    edge_copies = edges_start(0)
    arrived(edge_copies)
    share_copies = smooth_share(0)

    arrived(part_2)
    coarse_rows(2)
    arrived(part_3)
    coarse_rows(3)
    contract(1)
    sum_copies_b = sum_start(1)

    arrived(share_copies)
    expand(0)
    spread_0 = spread_start(0)
    spread_1 = spread_start(1)
    arrived(sum_copies_b)
    edge_copies_b = edges_start(1)
    arrived(edge_copies_b)
    share_copies_b = smooth_share(1)
    arrived(spread_0)
    back_0 = back_start(0)
    arrived(spread_1)
    back_1 = back_start(1)
    norm_copies = []
    for d in (2, 1, 3):
        copy = pltpu.make_async_remote_copy(
            src_ref=norm,
            dst_ref=norm_in.at[d - 1],
            send_sem=norm_send.at[d - 1],
            recv_sem=norm_recv.at[d - 1],
            device_id={"slot": (slot + d) % SLOTS},
            device_id_type=MESH,
        )
        copy.start()
        norm_copies.append(copy)
    arrived(share_copies_b)
    expand(1)
    spread_2 = spread_start(2)
    spread_3 = spread_start(3)
    spread_4 = spread_start(4)
    spread_5 = spread_start(5)
    arrived(norm_copies)
    norm_sum[...] = norm[...] + norm_in[0] + norm_in[1] + norm_in[2]
    last_copies = []
    for i, p in enumerate(partners):
        copy = pltpu.make_async_remote_copy(
            src_ref=norm_sum,
            dst_ref=norm_all.at[me],
            send_sem=last_send.at[i],
            recv_sem=last_recv.at[i],
            device_id={"region": p},
            device_id_type=MESH,
        )
        copy.start()
        last_copies.append(copy)
    norm_all[me] = norm_sum[...]

    arrived(spread_2)
    back_2 = back_start(2)
    arrived(spread_3)
    back_3 = back_start(3)
    arrived(spread_4)
    back_4 = back_start(4)
    arrived(spread_5)
    back_5 = back_start(5)

    arrived(back_0)
    fine_rows(0)
    arrived(back_1)
    fine_rows(1)
    arrived(last_copies)
    sums = jnp.sum(jnp.sum(norm_all[...], axis=0), axis=1, keepdims=True)
    squares = jnp.broadcast_to(sums, (8, COARSE))
    step = squares / (squares + pltpu.roll(squares, 6, 0))
    step_ref[...] = step
    arrived(back_2)
    fine_rows(2)
    stores = store_start(0)
    arrived(back_3)
    fine_rows(3)
    arrived(back_4)
    fine_rows(4)
    arrived(back_5)
    fine_rows(5)
    stores += store_start(1)
    for copies in (
        index_copies,
        out_2,
        out_3,
        part_0,
        part_1,
        part_2,
        part_3,
        sum_copies,
        sum_copies_b,
        edge_copies,
        edge_copies_b,
        share_copies,
        share_copies_b,
        norm_copies,
        last_copies,
        spread_0,
        spread_1,
        spread_2,
        spread_3,
        spread_4,
        spread_5,
        back_0,
        back_1,
        back_2,
        back_3,
        back_4,
        back_5,
    ):
        for copy in copies:
            copy.wait_send()
    for copy in stores:
        copy.wait()


def per_device(residual, perturb, vertical_modes, column_weight, owner_table, column_map):
    vmem, dma = pltpu.VMEM, pltpu.SemaphoreType.DMA
    resid_part = residual[0].transpose(1, 0, 2)
    weight = column_weight.reshape(1, FINE)
    whole = pl.BlockSpec(memory_space=pltpu.VMEM)
    anywhere = pl.BlockSpec(memory_space=pl.ANY)
    n = len(HOPS)
    increment, step = pl.pallas_call(
        kernel,
        out_shape=(
            jax.ShapeDtypeStruct((FEAT, 2, FINE), F32),
            jax.ShapeDtypeStruct((8, COARSE), F32),
        ),
        in_specs=[whole] * 4 + [anywhere] * 2,
        out_specs=(anywhere, whole),
        scratch_shapes=[
            vmem((2, FEAT, FINE), F32),
            vmem((FEAT_PAD, MEMBERS, COARSE), BF16),
            vmem((WIDE, FINE), F32),
            vmem((FINE, WIDE), BF16),
            vmem((2, REGIONS * CAP, FINE), BF16),
            vmem((2, FINE, REGIONS * CAP), BF16),
            vmem((2, 8, 16, COARSE), BF16),
            vmem((2, 8, 16, COARSE), BF16),
            vmem((2, 4, 8 * CAP, COARSE), BF16),
            vmem((2, 4, COARSE, 8 * CAP), BF16),
            [vmem((8, 4, CAP, width), BF16) for _, width, _ in OUT],
            [vmem((4, 8, CAP, width), BF16) for _, width, _ in OUT],
            [vmem((4, COARSE, width), BF16) for _, width, _ in OUT],
            [vmem((4, COARSE, width), BF16) for _, width, _ in OUT],
            vmem((WIDE, COARSE), F32),
            vmem((FEAT_PAD, 2 * SPREAD), F32),
            vmem((FEAT_PAD * GROUP, 2 * SPREAD), BF16),
            vmem((2 * SPREAD, FEAT_PAD * GROUP), BF16),
            vmem((SPREAD, GROUPS * COARSE), F32),
            vmem((2 * SPREAD, GROUPS * COARSE), BF16),
            vmem((2 * ROWS, COARSE), F32),
            vmem((2, SLOTS - 1, SHARE, COARSE), F32),
            vmem((2, 2, 40, COARSE), F32),
            vmem((2, 2, 40, COARSE), F32),
            vmem((2, SHARE, COARSE), F32),
            vmem((2, SLOTS, SHARE, COARSE), BF16),
            vmem((WIDE, COARSE), F32),
            [vmem((COARSE, width), BF16) for _, width, _ in BACK],
            [vmem((4, COARSE, width), BF16) for _, width, _ in BACK],
            [vmem((8, 4, CAP, width), BF16) for _, width, _ in BACK],
            [vmem((8, 4, CAP, width), BF16) for _, width, _ in BACK],
            vmem((2, FEAT, FINE), F32),
            vmem((8, COARSE), F32),
            vmem((SLOTS - 1, 8, COARSE), F32),
            vmem((8, COARSE), F32),
            vmem((REGIONS, 8, COARSE), F32),
            dma((3,)),
            *[dma((rows, cols)) for rows, cols in ((2, 7), (4, 7), (4, 3), (6, 3), (6, 7)) for _ in range(2)],
            dma((2, 3)),
            dma((2, 3)),
            dma((2, 2)),
            dma((2, 2)),
            dma((2, 3)),
            dma((2, 3)),
            dma((3,)),
            dma((3,)),
            dma((n,)),
            dma((n,)),
        ],
        compiler_params=pltpu.CompilerParams(
            collective_id=0, has_side_effects=True, vmem_limit_bytes=60 * 2**20
        ),
        name="hessian",
    )(
        owner_table.reshape(1, REGIONS * FINE),
        column_map.reshape(1, REGIONS * FINE),
        weight,
        vertical_modes.T,
        resid_part,
        perturb[0].transpose(1, 0, 2),
    )
    step_length = step[0:2, 0]
    product = resid_part + increment * column_weight[None, None, :]
    next_residual = resid_part - step_length[None, :, None] * product
    return (product.transpose(1, 0, 2)[None], step_length, next_residual.transpose(1, 0, 2)[None])


def solution(mesh):
    in_specs = (
        P("slot", None, None, "region"),
        P("slot", None, None, "region"),
        P(),
        P("region"),
        P(),
        P(),
    )
    out_specs = (P("slot", None, None, "region"), P(), P("slot", None, None, "region"))
    return jax.shard_map(
        per_device, mesh=mesh, in_specs=in_specs, out_specs=out_specs, check_vma=False
    )
```

```python
import jax
import jax.numpy as jnp
from jax import lax
from jax.experimental import pallas as pl
from jax.experimental.pallas import tpu as pltpu
from jax.sharding import PartitionSpec as P

MESH = pl.DeviceIdType.MESH
LAT_ROWS = 8
DIFFUSION_RATE = 0.2
F32 = jnp.float32
BF16 = jnp.bfloat16

REGIONS = 32
CAP = 32
SLOTS = 4
FINE = 512
COARSE = 128
FEAT = 685
FEAT_PAD = 704
WIDE = 1408
MEMBERS = 64
MODES = 10
ROWS = MODES * MEMBERS
SHARE = ROWS // SLOTS
OUT = ((0, 384, 0), (384, 384, 1), (768, 384, 0), (1152, 256, 1))
BACK = ((0, 384, 0), (384, 256, 1), (640, 256, 0), (896, 256, 1), (1152, 128, 0), (1280, 128, 1))
LINE = ((2, 0), (2, 1), (1, 0), (3, 0), (1, 1), (3, 1), (0, 1))
GROUP = 8
GROUPS = MEMBERS // GROUP
SPREAD = MODES * GROUP
STEP = 176

NEAR_FIRST = (
    [(0, 1), (1, 0), (0, 3), (3, 0)],
    [(1, 1), (3, 3), (1, 3), (3, 1)],
    [(2, 0), (0, 2)],
    [(2, 1), (1, 2), (2, 3), (3, 2)],
    [(2, 2)],
)
HOPS = [(z, x, c) for group in NEAR_FIRST[::-1] for c in (0, 1) for z, x in group] + [(0, 0, 1)]


def smooth(cells, west_from, east_from):
    lane = lax.broadcasted_iota(jnp.int32, cells.shape, 1)
    row = lane % LAT_ROWS
    west = pltpu.roll(jnp.where(lane >= COARSE - LAT_ROWS, west_from, cells), LAT_ROWS, 1)
    east = pltpu.roll(jnp.where(lane < LAT_ROWS, east_from, cells), COARSE - LAT_ROWS, 1)
    south = pltpu.roll(cells, 1, 1)
    north = pltpu.roll(cells, COARSE - 1, 1)
    along = jnp.where(row > 0, south - cells, 0.0) + jnp.where(row < LAT_ROWS - 1, north - cells, 0.0)
    return cells + DIFFUSION_RATE * (west + east - 2.0 * cells + along)


def dot(a, b):
    return jnp.dot(a, b, preferred_element_type=F32)


def kernel(
    owners_ref,
    map_ref,
    weight_ref,
    modes_ref,
    resid_hbm,
    members_hbm,
    fine_hbm,
    step_ref,
    resid,
    members,
    wide_rows,
    wide_cols,
    slot_hot_t,
    slot_hot,
    index_out,
    index_in,
    place,
    place_t,
    send,
    middle,
    part,
    part_in,
    coarse,
    modes_rep,
    mixer,
    mixer_t,
    gathered_modes,
    mode_cells,
    control,
    summed_in,
    edge_out,
    edge_in,
    shares,
    gathered,
    total,
    spread_out,
    spread_in,
    back,
    home,
    fine,
    norm,
    norm_in,
    norm_sum,
    norm_all,
    load_sem,
    index_send,
    index_recv,
    out_send,
    out_recv,
    part_send,
    part_recv,
    spread_send,
    spread_recv,
    back_send,
    back_recv,
    sum_send,
    sum_recv,
    edge_send,
    edge_recv,
    share_send,
    share_recv,
    norm_send,
    norm_recv,
    last_send,
    last_recv,
):
    me = lax.axis_index("region")
    slot = lax.axis_index("slot")
    z, x, core = me // 8, (me // 2) % 4, me % 2

    def region_at(hop):
        dz, dx, dc = hop
        return (((z + dz) % 4) * 4 + (x + dx) % 4) * 2 + (core + dc) % 2

    partners = [region_at(h) for h in HOPS]
    load_resid = [pltpu.make_async_copy(resid_hbm.at[:, v, :], resid.at[v], load_sem.at[v]) for v in range(2)]
    for copy in load_resid:
        copy.start()

    barrier = pltpu.get_barrier_semaphore()
    for p in partners:
        pl.semaphore_signal(barrier, inc=1, device_id={"region": p}, device_id_type=MESH)
    for d in (1, 2, 3):
        pl.semaphore_signal(barrier, inc=1, device_id={"slot": (slot + d) % SLOTS}, device_id_type=MESH)

    mine = pl.ds(pl.multiple_of(me * FINE, FINE), FINE)
    own = owners_ref[:, mine]
    owner_hot = (lax.broadcasted_iota(jnp.int32, (REGIONS, FINE), 0) == own).astype(BF16)
    earlier = (
        lax.broadcasted_iota(jnp.int32, (FINE, FINE), 0) < lax.broadcasted_iota(jnp.int32, (FINE, FINE), 1)
    ).astype(BF16)
    before = dot(owner_hot, earlier)
    rank = jnp.sum(owner_hot.astype(F32) * before, axis=0, keepdims=True)
    rank = rank.astype(jnp.int32)
    own_z, own_x, own_core = own // 8, (own // 2) % 4, own % 2
    index_row = (map_ref[:, mine] + 1).astype(F32)
    index_rows = jnp.broadcast_to(index_row, (16, FINE)).astype(BF16)
    for mode, (first, second) in enumerate(((own_z, own_x), (own_x, own_z))):
        my_slots = (first * 2 + own_core) * 128 + second * CAP + rank
        for q in range(4):
            hot = lax.broadcasted_iota(jnp.int32, (256, FINE), 0) + q * 256 == my_slots
            hot = hot.astype(F32).astype(BF16)
            slot_hot_t[mode, pl.ds(q * 256, 256), :] = hot
            got = lax.dot_general(
                index_rows, hot, (((1,), (1,)), ((), ())), preferred_element_type=F32
            ).astype(BF16)
            for e in range(2):
                index_out[mode, 2 * q + e] = got[:, e * 128 : (e + 1) * 128]

    spare = FEAT_PAD - FEAT
    wide_rows[pl.ds(FEAT, spare), :] = jnp.zeros((spare, FINE), F32)
    wide_rows[pl.ds(FEAT_PAD + FEAT, spare), :] = jnp.zeros((spare, FINE), F32)
    pl.semaphore_wait(barrier, len(HOPS) + 3)

    def spot(mode):
        return (z, x) if mode == 0 else (x, z)

    def device_at(mode, a, b, c):
        return ((a * 4 + b) if mode == 0 else (b * 4 + a)) * 2 + c

    def push(source, landing, send_sem, recv_sem, target):
        copy = pltpu.make_async_remote_copy(
            src_ref=source,
            dst_ref=landing,
            send_sem=send_sem,
            recv_sem=recv_sem,
            device_id=target,
            device_id_type=MESH,
        )
        copy.start()
        return copy

    def line_peers(mode):
        a, b = spot(mode)
        for j, (da, dc) in enumerate(LINE):
            a_to, c_to = (a + da) % 4, (core + dc) % 2
            yield j, a_to * 2 + c_to, {"region": device_at(mode, a_to, b, c_to)}

    def cross_peers(mode):
        a, b = spot(mode)
        for j, db in enumerate((2, 1, 3)):
            b_to = (b + db) % 4
            yield j, b_to, {"region": device_at(mode, a, b_to, core)}

    def weigh(v):
        load_resid[v].wait()
        wide_rows[pl.ds(v * FEAT_PAD, FEAT), :] = resid[v] * weight_ref[...]

    def pack(piece):
        left, width, mode = OUT[piece]
        for q in range(4):
            cols = slice(q * 128, (q + 1) * 128)
            wide_cols[cols, left : left + width] = wide_rows[left : left + width, cols].T.astype(BF16)

        def one(q, carry):
            rows = slot_hot_t[mode, pl.ds(pl.multiple_of(q * 256, 256), 256), :]
            got = dot(rows, wide_cols[:, left : left + width])
            send[piece][pl.ds(q * 2, 2)] = got.astype(BF16).reshape(2, 4, CAP, width)
            return carry

        lax.fori_loop(0, 4, one, 0)

    def out_start(piece, ahead):
        mode = OUT[piece][2]
        here = spot(mode)[0] * 2 + core
        copies = []
        for j, there, target in line_peers(mode):
            if ahead is not None:
                ahead[j].wait_send()
            copies.append(
                push(
                    send[piece].at[there],
                    middle[piece].at[:, here],
                    out_send.at[piece, j],
                    out_recv.at[piece, j],
                    target,
                )
            )
        middle[piece][:, here] = send[piece][here]
        return copies

    def part_start(piece):
        mode = OUT[piece][2]
        here = spot(mode)[1]
        for b in range(4):
            rows = middle[piece][b].reshape(8 * CAP, OUT[piece][1])
            part[piece][b] = dot(place_t[mode, b], rows).astype(BF16)
        copies = [
            push(
                part[piece].at[there],
                part_in[piece].at[here],
                part_send.at[piece, j],
                part_recv.at[piece, j],
                target,
            )
            for j, there, target in cross_peers(mode)
        ]
        part_in[piece][here] = part[piece][here]
        return copies

    def coarse_rows(piece):
        left, width, _ = OUT[piece]
        sums = part_in[piece][0].astype(F32)
        for b in range(1, 4):
            sums = sums + part_in[piece][b].astype(F32)
        coarse[pl.ds(left, width), :] = sums.T

    index_copies = []
    for mode in range(2):
        here = spot(mode)[0] * 2 + core
        for j, there, target in line_peers(mode):
            index_copies.append(
                push(
                    index_out.at[mode, there],
                    index_in.at[mode, here],
                    index_send.at[mode, j],
                    index_recv.at[mode, j],
                    target,
                )
            )
        index_in[mode, here] = index_out[mode, here]
    weigh(0)
    pack(0)
    out_0 = out_start(0, None)
    weigh(1)
    load_members = pltpu.make_async_copy(members_hbm, members.at[pl.ds(0, FEAT)], load_sem.at[2])
    load_members.start()
    pack(1)
    out_1 = out_start(1, None)
    pack(2)
    pack(3)

    norm[...] = jnp.zeros_like(norm)
    for v in range(2):
        by_col = jnp.sum(resid[v] * resid[v], axis=0, keepdims=True)
        norm[pl.ds(v, 1), :] = by_col[:, 0:128] + by_col[:, 128:256] + by_col[:, 256:384] + by_col[:, 384:512]
    for mode in range(2):
        slot_hot[mode] = slot_hot_t[mode].T
    members[pl.ds(FEAT, spare)] = jnp.zeros((spare, MEMBERS, COARSE), BF16)

    repeat = (
        lax.broadcasted_iota(jnp.int32, (SPREAD, MODES), 0) // GROUP
        == lax.broadcasted_iota(jnp.int32, (SPREAD, MODES), 1)
    ).astype(F32).astype(BF16)
    high = modes_ref[...].astype(BF16)
    low = (modes_ref[...] - high.astype(F32)).astype(BF16)
    modes_rep[...] = jnp.zeros_like(modes_rep)
    modes_rep[pl.ds(0, FEAT), :] = jnp.concatenate([dot(repeat, high), dot(repeat, low)], axis=0).T

    def mixer_step(i, carry):
        cut = (32, GROUP, 2 * SPREAD)
        rows = modes_rep[pl.ds(pl.multiple_of(i * 32, 32), 32), :]
        same = lax.broadcasted_iota(jnp.int32, cut, 1) == lax.broadcasted_iota(jnp.int32, cut, 2) % GROUP
        block = jnp.where(same, jnp.broadcast_to(rows[:, None, :], cut), 0.0).reshape(256, 2 * SPREAD)
        at = pl.ds(pl.multiple_of(i * 256, 256), 256)
        mixer[at, :] = block.astype(BF16)
        mixer_t[:, at] = block.T.astype(BF16)
        return carry

    lax.fori_loop(0, FEAT_PAD // 32, mixer_step, 0)

    for copy in index_copies:
        copy.wait_recv()
    lane = lax.broadcasted_iota(jnp.int32, (8, COARSE), 1)
    for mode in range(2):
        tables = [index_in[mode, p].astype(F32)[0:8] for p in range(8)]
        for b in range(4):
            halves = []
            for h in range(2):
                row = jnp.zeros((8, COARSE), F32)
                for g in range(4):
                    shift = (g - b) * CAP % COARSE
                    table = tables[h * 4 + g]
                    row = jnp.where(lane // CAP == g, pltpu.roll(table, shift, 1) if shift else table, row)
                halves.append(row[0:1])
            row = jnp.concatenate(halves, axis=1)
            hot = (lax.broadcasted_iota(jnp.int32, (COARSE, 8 * CAP), 0) + 1).astype(F32) == row
            hot = hot.astype(F32)
            place_t[mode, b] = hot.astype(BF16)
            place[mode, b] = hot.T.astype(BF16)
    load_members.wait()

    def contract(v):
        gathered_modes[...] = jnp.zeros_like(gathered_modes)

        def chunk(i, carry):
            field = coarse[pl.ds(pl.multiple_of(v * FEAT_PAD + i * STEP, STEP), STEP), :]
            cells = members[pl.ds(i * STEP, STEP)].astype(F32).reshape(STEP, GROUPS, GROUP, COARSE)
            product = cells * field[:, None, None, :]
            left = mixer_t[:, pl.ds(pl.multiple_of(i * STEP * GROUP, STEP * GROUP), STEP * GROUP)]
            for pair in range(GROUPS // 2):
                both = jnp.concatenate(
                    [product[:, 2 * pair + e].reshape(STEP * GROUP, COARSE) for e in range(2)], axis=1
                )
                top = both.astype(BF16)
                rest = (both - top.astype(F32)).astype(BF16)
                main = dot(left, top)
                gathered_modes[:, pair * 256 : (pair + 1) * 256] += (
                    main[0:SPREAD] + main[SPREAD:] + dot(left[0:SPREAD], rest)
                )
            return carry

        lax.fori_loop(0, FEAT_PAD // STEP, chunk, 0)
        for m in range(MODES):
            for g in range(GROUPS):
                control[pl.ds(v * ROWS + m * MEMBERS + g * GROUP, GROUP), :] = gathered_modes[
                    m * GROUP : (m + 1) * GROUP, g * COARSE : (g + 1) * COARSE
                ]

    def share_rows(v, t):
        return pl.ds(pl.multiple_of(v * ROWS + t * SHARE, 8), SHARE)

    def sum_start(v):
        copies = []
        for d in (2, 1, 3):
            t = (slot + d) % SLOTS
            copy = pltpu.make_async_remote_copy(
                src_ref=control.at[share_rows(v, t)],
                dst_ref=summed_in.at[v, d - 1],
                send_sem=sum_send.at[v, d - 1],
                recv_sem=sum_recv.at[v, d - 1],
                device_id={"slot": t},
                device_id_type=MESH,
            )
            copy.start()
            copies.append(copy)
        return copies

    def edges_start(v):
        cells = control[share_rows(v, slot), :]
        for d in range(3):
            cells = cells + summed_in[v, d]
        shares[v] = cells
        lane = lax.broadcasted_iota(jnp.int32, (40, COARSE), 1)
        east = jnp.zeros((40, COARSE), F32)
        west = jnp.zeros((40, COARSE), F32)
        for g in range(4):
            part = cells[g * 40 : (g + 1) * 40]
            mine = lane // 16 == g
            east = jnp.where(mine, pltpu.roll(part, 16 * g + 16, 1), east)
            west = jnp.where(mine, pltpu.roll(part, 16 * g, 1) if g else part, west)
        edge_out[v, 0] = east
        edge_out[v, 1] = west
        copies = []
        for side, p in ((0, (me + 1) % REGIONS), (1, (me + REGIONS - 1) % REGIONS)):
            copy = pltpu.make_async_remote_copy(
                src_ref=edge_out.at[v, side],
                dst_ref=edge_in.at[v, side],
                send_sem=edge_send.at[v, side],
                recv_sem=edge_recv.at[v, side],
                device_id={"region": p},
                device_id_type=MESH,
            )
            copy.start()
            copies.append(copy)
        return copies

    def smooth_share(v):
        cells = shares[v]
        lane = lax.broadcasted_iota(jnp.int32, (SHARE, COARSE), 1)
        west = jnp.concatenate([pltpu.roll(edge_in[v, 0], 112 - 16 * g, 1) for g in range(4)], axis=0)
        east = jnp.concatenate(
            [pltpu.roll(edge_in[v, 1], 128 - 16 * g, 1) if g else edge_in[v, 1] for g in range(4)], axis=0
        )
        once = smooth(cells, west, east)
        west = jnp.where(lane < LAT_ROWS, cells, west)
        east = jnp.where(lane >= COARSE - LAT_ROWS, cells, east)
        twice = smooth(once, smooth(west, west, west), smooth(east, east, east))
        norm[pl.ds(2 + v, 1), :] = jnp.sum(once * once, axis=0, keepdims=True)
        smooth_bits = twice.astype(BF16)
        gathered[v, slot] = smooth_bits
        copies = []
        for d in (2, 1, 3):
            copy = pltpu.make_async_remote_copy(
                src_ref=gathered.at[v, slot],
                dst_ref=gathered.at[v, slot],
                send_sem=share_send.at[v, d - 1],
                recv_sem=share_recv.at[v, d - 1],
                device_id={"slot": (slot + d) % SLOTS},
                device_id_type=MESH,
            )
            copy.start()
            copies.append(copy)
        return copies

    def expand(v):
        every = jnp.concatenate([gathered[v, t].astype(F32) for t in range(SLOTS)], axis=0)
        for g in range(GROUPS):
            cells = jnp.concatenate(
                [every[m * MEMBERS + g * GROUP : m * MEMBERS + (g + 1) * GROUP] for m in range(MODES)], axis=0
            ).astype(BF16)
            mode_cells[0:SPREAD, g * COARSE : (g + 1) * COARSE] = cells
            mode_cells[SPREAD:, g * COARSE : (g + 1) * COARSE] = cells

        def chunk(i, carry):
            left = mixer[pl.ds(pl.multiple_of(i * STEP * GROUP, STEP * GROUP), STEP * GROUP), :]
            cells = members[pl.ds(i * STEP, STEP)].astype(F32).reshape(STEP, GROUPS, GROUP, COARSE)
            sums = jnp.zeros((STEP, GROUP, COARSE), F32)
            for pair in range(GROUPS // 2):
                mixed = dot(left, mode_cells[:, pair * 256 : (pair + 1) * 256])
                for e in range(2):
                    part = mixed[:, e * COARSE : (e + 1) * COARSE].reshape(STEP, GROUP, COARSE)
                    sums = sums + cells[:, 2 * pair + e] * part
            at = pl.ds(pl.multiple_of(v * FEAT_PAD + i * STEP, STEP), STEP)
            total[at, :] = jnp.sum(sums, axis=1)
            return carry

        lax.fori_loop(0, FEAT_PAD // STEP, chunk, 0)

    def arrived(copies):
        for copy in copies:
            copy.wait_recv()

    def spread_start(piece):
        left, width, mode = BACK[piece]
        here = spot(mode)[1]
        spread_out[piece][...] = total[pl.ds(left, width), :].T.astype(BF16)
        copies = [
            push(
                spread_out[piece],
                spread_in[piece].at[here],
                spread_send.at[piece, j],
                spread_recv.at[piece, j],
                target,
            )
            for j, _, target in cross_peers(mode)
        ]
        spread_in[piece][here] = spread_out[piece][...]
        return copies

    def back_start(piece):
        _, width, mode = BACK[piece]
        here = spot(mode)[0] * 2 + core
        for b in range(4):
            rows = dot(place[mode, b], spread_in[piece][b])
            back[piece][:, b] = rows.astype(BF16).reshape(8, CAP, width)
        copies = [
            push(
                back[piece].at[there],
                home[piece].at[here],
                back_send.at[piece, j],
                back_recv.at[piece, j],
                target,
            )
            for j, there, target in line_peers(mode)
        ]
        home[piece][here] = back[piece][here]
        return copies

    def fine_rows(piece):
        left, width, mode = BACK[piece]
        source = home[piece][...].reshape(REGIONS * CAP, width)
        for q in range(4):
            cols = slice(q * 128, (q + 1) * 128)
            rows = dot(slot_hot[mode, pl.ds(q * 128, 128), :], source).T
            for v in range(2):
                first = max(left, v * FEAT_PAD)
                last = min(left + width, v * FEAT_PAD + FEAT)
                if first < last:
                    fine[v, first - v * FEAT_PAD : last - v * FEAT_PAD, cols] = rows[first - left : last - left]

    def store_start(v):
        copies = [pltpu.make_async_copy(fine.at[v], fine_hbm.at[:, v, :], load_sem.at[v])]
        for copy in copies:
            copy.start()
        return copies

    arrived(out_0)
    part_0 = part_start(0)
    arrived(out_1)
    part_1 = part_start(1)
    out_2 = out_start(2, out_0)
    out_3 = out_start(3, out_1)
    total[pl.ds(FEAT_PAD, FEAT_PAD), :] = jnp.zeros((FEAT_PAD, COARSE), F32)
    arrived(part_0)
    coarse_rows(0)
    arrived(part_1)
    coarse_rows(1)
    contract(0)
    sum_copies = sum_start(0)
    arrived(out_2)
    part_2 = part_start(2)
    arrived(out_3)
    part_3 = part_start(3)
    arrived(sum_copies)
    edge_copies = edges_start(0)
    arrived(edge_copies)
    share_copies = smooth_share(0)

    arrived(part_2)
    coarse_rows(2)
    arrived(part_3)
    coarse_rows(3)
    contract(1)
    sum_copies_b = sum_start(1)

    arrived(share_copies)
    expand(0)
    spread_0 = spread_start(0)
    spread_1 = spread_start(1)
    arrived(sum_copies_b)
    edge_copies_b = edges_start(1)
    arrived(edge_copies_b)
    share_copies_b = smooth_share(1)
    arrived(spread_0)
    back_0 = back_start(0)
    arrived(spread_1)
    back_1 = back_start(1)
    norm_copies = []
    for d in (2, 1, 3):
        copy = pltpu.make_async_remote_copy(
            src_ref=norm,
            dst_ref=norm_in.at[d - 1],
            send_sem=norm_send.at[d - 1],
            recv_sem=norm_recv.at[d - 1],
            device_id={"slot": (slot + d) % SLOTS},
            device_id_type=MESH,
        )
        copy.start()
        norm_copies.append(copy)
    arrived(share_copies_b)
    expand(1)
    spread_2 = spread_start(2)
    spread_3 = spread_start(3)
    spread_4 = spread_start(4)
    spread_5 = spread_start(5)
    arrived(norm_copies)
    norm_sum[...] = norm[...] + norm_in[0] + norm_in[1] + norm_in[2]
    last_copies = []
    for i, p in enumerate(partners):
        copy = pltpu.make_async_remote_copy(
            src_ref=norm_sum,
            dst_ref=norm_all.at[me],
            send_sem=last_send.at[i],
            recv_sem=last_recv.at[i],
            device_id={"region": p},
            device_id_type=MESH,
        )
        copy.start()
        last_copies.append(copy)
    norm_all[me] = norm_sum[...]

    arrived(spread_2)
    back_2 = back_start(2)
    arrived(spread_3)
    back_3 = back_start(3)
    arrived(spread_4)
    back_4 = back_start(4)
    arrived(spread_5)
    back_5 = back_start(5)

    arrived(back_0)
    fine_rows(0)
    arrived(back_1)
    fine_rows(1)
    arrived(last_copies)
    sums = jnp.sum(jnp.sum(norm_all[...], axis=0), axis=1, keepdims=True)
    squares = jnp.broadcast_to(sums, (8, COARSE))
    step = squares / (squares + pltpu.roll(squares, 6, 0))
    step_ref[...] = step
    arrived(back_2)
    fine_rows(2)
    stores = store_start(0)
    arrived(back_3)
    fine_rows(3)
    arrived(back_4)
    fine_rows(4)
    arrived(back_5)
    fine_rows(5)
    stores += store_start(1)
    for copies in (
        index_copies,
        out_2,
        out_3,
        part_0,
        part_1,
        part_2,
        part_3,
        sum_copies,
        sum_copies_b,
        edge_copies,
        edge_copies_b,
        share_copies,
        share_copies_b,
        norm_copies,
        last_copies,
        spread_0,
        spread_1,
        spread_2,
        spread_3,
        spread_4,
        spread_5,
        back_0,
        back_1,
        back_2,
        back_3,
        back_4,
        back_5,
    ):
        for copy in copies:
            copy.wait_send()
    for copy in stores:
        copy.wait()


def last_step(resid_ref, increment_ref, weight_ref, step_ref, product_ref, next_ref, length_ref):
    cut = (resid_ref.shape[0] // 8, 8, COARSE)
    row = lax.broadcasted_iota(jnp.int32, (8, COARSE), 0)
    step = jnp.where(row % 2 == 1, step_ref[1:2, :], step_ref[0:1, :])
    weight = weight_ref[:, 0:COARSE]
    for j in range(1, 4):
        weight = jnp.where(row // 2 == j, weight_ref[:, j * COARSE : (j + 1) * COARSE], weight)
    for v in range(2):
        length_ref[v] = jnp.max(step_ref[v : v + 1, :])
    resid = resid_ref[...].reshape(cut)
    product = resid + increment_ref[...].reshape(cut) * weight[None]
    product_ref[...] = product.reshape(resid_ref.shape)
    next_ref[...] = (resid - step[None] * product).reshape(resid_ref.shape)


def by_lanes(fields):
    return fields.reshape(FEAT, 2, 4, COARSE).transpose(0, 2, 1, 3).reshape(FEAT * 8, COARSE)


def by_fields(rows):
    return rows.reshape(FEAT, 4, 2, COARSE).transpose(2, 0, 1, 3).reshape(1, 2, FEAT, FINE)


def per_device(residual, perturb, vertical_modes, column_weight, owner_table, column_map):
    vmem, dma = pltpu.VMEM, pltpu.SemaphoreType.DMA
    resid_part = residual[0].transpose(1, 0, 2)
    weight = column_weight.reshape(1, FINE)
    whole = pl.BlockSpec(memory_space=pltpu.VMEM)
    anywhere = pl.BlockSpec(memory_space=pl.ANY)
    n = len(HOPS)
    increment, step = pl.pallas_call(
        kernel,
        out_shape=(
            jax.ShapeDtypeStruct((FEAT, 2, FINE), F32),
            jax.ShapeDtypeStruct((8, COARSE), F32),
        ),
        in_specs=[whole] * 4 + [anywhere] * 2,
        out_specs=(anywhere, whole),
        scratch_shapes=[
            vmem((2, FEAT, FINE), F32),
            vmem((FEAT_PAD, MEMBERS, COARSE), BF16),
            vmem((WIDE, FINE), F32),
            vmem((FINE, WIDE), BF16),
            vmem((2, REGIONS * CAP, FINE), BF16),
            vmem((2, FINE, REGIONS * CAP), BF16),
            vmem((2, 8, 16, COARSE), BF16),
            vmem((2, 8, 16, COARSE), BF16),
            vmem((2, 4, 8 * CAP, COARSE), BF16),
            vmem((2, 4, COARSE, 8 * CAP), BF16),
            [vmem((8, 4, CAP, width), BF16) for _, width, _ in OUT],
            [vmem((4, 8, CAP, width), BF16) for _, width, _ in OUT],
            [vmem((4, COARSE, width), BF16) for _, width, _ in OUT],
            [vmem((4, COARSE, width), BF16) for _, width, _ in OUT],
            vmem((WIDE, COARSE), F32),
            vmem((FEAT_PAD, 2 * SPREAD), F32),
            vmem((FEAT_PAD * GROUP, 2 * SPREAD), BF16),
            vmem((2 * SPREAD, FEAT_PAD * GROUP), BF16),
            vmem((SPREAD, GROUPS * COARSE), F32),
            vmem((2 * SPREAD, GROUPS * COARSE), BF16),
            vmem((2 * ROWS, COARSE), F32),
            vmem((2, SLOTS - 1, SHARE, COARSE), F32),
            vmem((2, 2, 40, COARSE), F32),
            vmem((2, 2, 40, COARSE), F32),
            vmem((2, SHARE, COARSE), F32),
            vmem((2, SLOTS, SHARE, COARSE), BF16),
            vmem((WIDE, COARSE), F32),
            [vmem((COARSE, width), BF16) for _, width, _ in BACK],
            [vmem((4, COARSE, width), BF16) for _, width, _ in BACK],
            [vmem((8, 4, CAP, width), BF16) for _, width, _ in BACK],
            [vmem((8, 4, CAP, width), BF16) for _, width, _ in BACK],
            vmem((2, FEAT, FINE), F32),
            vmem((8, COARSE), F32),
            vmem((SLOTS - 1, 8, COARSE), F32),
            vmem((8, COARSE), F32),
            vmem((REGIONS, 8, COARSE), F32),
            dma((3,)),
            *[dma((rows, cols)) for rows, cols in ((2, 7), (4, 7), (4, 3), (6, 3), (6, 7)) for _ in range(2)],
            dma((2, 3)),
            dma((2, 3)),
            dma((2, 2)),
            dma((2, 2)),
            dma((2, 3)),
            dma((2, 3)),
            dma((3,)),
            dma((3,)),
            dma((n,)),
            dma((n,)),
        ],
        compiler_params=pltpu.CompilerParams(
            collective_id=0, has_side_effects=True, vmem_limit_bytes=60 * 2**20
        ),
        name="hessian",
    )(
        owner_table.reshape(1, REGIONS * FINE),
        column_map.reshape(1, REGIONS * FINE),
        weight,
        vertical_modes.T,
        resid_part,
        perturb[0].transpose(1, 0, 2),
    )
    rows = FEAT // 5 * 8
    block = pl.BlockSpec((rows, COARSE), lambda i: (i, 0))
    small = pl.BlockSpec((8, COARSE), lambda i: (0, 0))
    product, next_residual, step_length = pl.pallas_call(
        last_step,
        grid=(5,),
        out_shape=(jax.ShapeDtypeStruct((FEAT * 8, COARSE), F32),) * 2 + (jax.ShapeDtypeStruct((2,), F32),),
        in_specs=[block, block, pl.BlockSpec((1, FINE), lambda i: (0, 0)), small],
        out_specs=(block, block, pl.BlockSpec(memory_space=pltpu.SMEM)),
        name="last_step",
    )(
        by_lanes(resid_part),
        by_lanes(increment),
        weight,
        step,
    )
    return (by_fields(product), step_length, by_fields(next_residual))


def solution(mesh):
    in_specs = (
        P("slot", None, None, "region"),
        P("slot", None, None, "region"),
        P(),
        P("region"),
        P(),
        P(),
    )
    out_specs = (P("slot", None, None, "region"), P(), P("slot", None, None, "region"))
    return jax.shard_map(
        per_device, mesh=mesh, in_specs=in_specs, out_specs=out_specs, check_vma=False
    )
```

```python
import jax
import jax.numpy as jnp
from jax import lax
from jax.experimental import pallas as pl
from jax.experimental.pallas import tpu as pltpu
from jax.sharding import PartitionSpec as P

MESH = pl.DeviceIdType.MESH
LAT_ROWS = 8
DIFFUSION_RATE = 0.2
F32 = jnp.float32
BF16 = jnp.bfloat16

REGIONS = 32
CAP = 32
SLOTS = 4
FINE = 512
COARSE = 128
FEAT = 685
FEAT_PAD = 704
WIDE = 1408
MEMBERS = 64
MODES = 10
ROWS = MODES * MEMBERS
SHARE = ROWS // SLOTS
OUT = ((0, 384, 0), (384, 384, 1), (768, 384, 0), (1152, 256, 1))
BACK = ((0, 384, 0), (384, 256, 1), (640, 256, 0), (896, 256, 1), (1152, 128, 0), (1280, 128, 1))
LINE = ((2, 0), (2, 1), (1, 0), (3, 0), (1, 1), (3, 1), (0, 1))
GROUP = 8
GROUPS = MEMBERS // GROUP
SPREAD = MODES * GROUP
STEP = 176
WIDE_STEP = 352

NEAR_FIRST = (
    [(0, 1), (1, 0), (0, 3), (3, 0)],
    [(1, 1), (3, 3), (1, 3), (3, 1)],
    [(2, 0), (0, 2)],
    [(2, 1), (1, 2), (2, 3), (3, 2)],
    [(2, 2)],
)
HOPS = [(z, x, c) for group in NEAR_FIRST[::-1] for c in (0, 1) for z, x in group] + [(0, 0, 1)]


def smooth(cells, west_from, east_from):
    lane = lax.broadcasted_iota(jnp.int32, cells.shape, 1)
    row = lane % LAT_ROWS
    west = pltpu.roll(jnp.where(lane >= COARSE - LAT_ROWS, west_from, cells), LAT_ROWS, 1)
    east = pltpu.roll(jnp.where(lane < LAT_ROWS, east_from, cells), COARSE - LAT_ROWS, 1)
    south = pltpu.roll(cells, 1, 1)
    north = pltpu.roll(cells, COARSE - 1, 1)
    along = jnp.where(row > 0, south - cells, 0.0) + jnp.where(row < LAT_ROWS - 1, north - cells, 0.0)
    return cells + DIFFUSION_RATE * (west + east - 2.0 * cells + along)


def dot(a, b):
    return jnp.dot(a, b, preferred_element_type=F32)


def kernel(
    owners_ref,
    map_ref,
    weight_ref,
    modes_ref,
    resid_hbm,
    members_hbm,
    fine_hbm,
    step_ref,
    resid,
    members,
    wide_rows,
    wide_cols,
    slot_hot_t,
    slot_hot,
    index_out,
    index_in,
    place,
    place_t,
    send,
    middle,
    part,
    part_in,
    coarse,
    modes_rep,
    mixer,
    mixer_t,
    gathered_modes,
    mode_cells,
    control,
    summed_in,
    edge_out,
    edge_in,
    shares,
    gathered,
    total,
    spread_out,
    spread_in,
    back,
    home,
    fine,
    norm,
    norm_in,
    norm_sum,
    norm_all,
    load_sem,
    index_send,
    index_recv,
    out_send,
    out_recv,
    part_send,
    part_recv,
    spread_send,
    spread_recv,
    back_send,
    back_recv,
    sum_send,
    sum_recv,
    edge_send,
    edge_recv,
    share_send,
    share_recv,
    norm_send,
    norm_recv,
    last_send,
    last_recv,
):
    me = lax.axis_index("region")
    slot = lax.axis_index("slot")
    z, x, core = me // 8, (me // 2) % 4, me % 2

    def region_at(hop):
        dz, dx, dc = hop
        return (((z + dz) % 4) * 4 + (x + dx) % 4) * 2 + (core + dc) % 2

    partners = [region_at(h) for h in HOPS]
    load_resid = [pltpu.make_async_copy(resid_hbm.at[:, v, :], resid.at[v], load_sem.at[v]) for v in range(2)]
    for copy in load_resid:
        copy.start()

    barrier = pltpu.get_barrier_semaphore()
    for p in partners:
        pl.semaphore_signal(barrier, inc=1, device_id={"region": p}, device_id_type=MESH)
    for d in (1, 2, 3):
        pl.semaphore_signal(barrier, inc=1, device_id={"slot": (slot + d) % SLOTS}, device_id_type=MESH)

    mine = pl.ds(pl.multiple_of(me * FINE, FINE), FINE)
    own = owners_ref[:, mine]
    owner_hot = (lax.broadcasted_iota(jnp.int32, (REGIONS, FINE), 0) == own).astype(BF16)
    earlier = (
        lax.broadcasted_iota(jnp.int32, (FINE, FINE), 0) < lax.broadcasted_iota(jnp.int32, (FINE, FINE), 1)
    ).astype(BF16)
    before = dot(owner_hot, earlier)
    rank = jnp.sum(owner_hot.astype(F32) * before, axis=0, keepdims=True)
    rank = rank.astype(jnp.int32)
    own_z, own_x, own_core = own // 8, (own // 2) % 4, own % 2
    index_row = (map_ref[:, mine] + 1).astype(F32)
    index_rows = jnp.broadcast_to(index_row, (16, FINE)).astype(BF16)
    for mode, (first, second) in enumerate(((own_z, own_x), (own_x, own_z))):
        my_slots = (first * 2 + own_core) * 128 + second * CAP + rank
        for q in range(4):
            hot = lax.broadcasted_iota(jnp.int32, (256, FINE), 0) + q * 256 == my_slots
            hot = hot.astype(F32).astype(BF16)
            slot_hot_t[mode, pl.ds(q * 256, 256), :] = hot
            got = lax.dot_general(
                index_rows, hot, (((1,), (1,)), ((), ())), preferred_element_type=F32
            ).astype(BF16)
            for e in range(2):
                index_out[mode, 2 * q + e] = got[:, e * 128 : (e + 1) * 128]

    spare = FEAT_PAD - FEAT
    wide_rows[pl.ds(FEAT, spare), :] = jnp.zeros((spare, FINE), F32)
    wide_rows[pl.ds(FEAT_PAD + FEAT, spare), :] = jnp.zeros((spare, FINE), F32)
    pl.semaphore_wait(barrier, len(HOPS) + 3)

    def spot(mode):
        return (z, x) if mode == 0 else (x, z)

    def device_at(mode, a, b, c):
        return ((a * 4 + b) if mode == 0 else (b * 4 + a)) * 2 + c

    def push(source, landing, send_sem, recv_sem, target):
        copy = pltpu.make_async_remote_copy(
            src_ref=source,
            dst_ref=landing,
            send_sem=send_sem,
            recv_sem=recv_sem,
            device_id=target,
            device_id_type=MESH,
        )
        copy.start()
        return copy

    def line_peers(mode):
        a, b = spot(mode)
        for j, (da, dc) in enumerate(LINE):
            a_to, c_to = (a + da) % 4, (core + dc) % 2
            yield j, a_to * 2 + c_to, {"region": device_at(mode, a_to, b, c_to)}

    def cross_peers(mode):
        a, b = spot(mode)
        for j, db in enumerate((2, 1, 3)):
            b_to = (b + db) % 4
            yield j, b_to, {"region": device_at(mode, a, b_to, core)}

    def weigh(v):
        load_resid[v].wait()
        wide_rows[pl.ds(v * FEAT_PAD, FEAT), :] = resid[v] * weight_ref[...]

    def pack(piece):
        left, width, mode = OUT[piece]
        for q in range(4):
            cols = slice(q * 128, (q + 1) * 128)
            wide_cols[cols, left : left + width] = wide_rows[left : left + width, cols].T.astype(BF16)

        def one(q, carry):
            rows = slot_hot_t[mode, pl.ds(pl.multiple_of(q * 256, 256), 256), :]
            got = dot(rows, wide_cols[:, left : left + width])
            send[piece][pl.ds(q * 2, 2)] = got.astype(BF16).reshape(2, 4, CAP, width)
            return carry

        lax.fori_loop(0, 4, one, 0)

    def out_start(piece, ahead):
        mode = OUT[piece][2]
        here = spot(mode)[0] * 2 + core
        copies = []
        for j, there, target in line_peers(mode):
            if ahead is not None:
                ahead[j].wait_send()
            copies.append(
                push(
                    send[piece].at[there],
                    middle[piece].at[:, here],
                    out_send.at[piece, j],
                    out_recv.at[piece, j],
                    target,
                )
            )
        middle[piece][:, here] = send[piece][here]
        return copies

    def part_start(piece):
        mode = OUT[piece][2]
        here = spot(mode)[1]
        for b in range(4):
            rows = middle[piece][b].reshape(8 * CAP, OUT[piece][1])
            part[piece][b] = dot(place_t[mode, b], rows).astype(BF16)
        copies = [
            push(
                part[piece].at[there],
                part_in[piece].at[here],
                part_send.at[piece, j],
                part_recv.at[piece, j],
                target,
            )
            for j, there, target in cross_peers(mode)
        ]
        part_in[piece][here] = part[piece][here]
        return copies

    def coarse_rows(piece):
        left, width, _ = OUT[piece]
        sums = part_in[piece][0].astype(F32)
        for b in range(1, 4):
            sums = sums + part_in[piece][b].astype(F32)
        coarse[pl.ds(left, width), :] = sums.T

    index_copies = []
    for mode in range(2):
        here = spot(mode)[0] * 2 + core
        for j, there, target in line_peers(mode):
            index_copies.append(
                push(
                    index_out.at[mode, there],
                    index_in.at[mode, here],
                    index_send.at[mode, j],
                    index_recv.at[mode, j],
                    target,
                )
            )
        index_in[mode, here] = index_out[mode, here]
    weigh(0)
    pack(0)
    out_0 = out_start(0, None)
    weigh(1)
    load_members = pltpu.make_async_copy(members_hbm, members.at[pl.ds(0, FEAT)], load_sem.at[2])
    load_members.start()
    pack(1)
    out_1 = out_start(1, None)
    pack(2)
    pack(3)

    norm[...] = jnp.zeros_like(norm)
    for v in range(2):
        by_col = jnp.sum(resid[v] * resid[v], axis=0, keepdims=True)
        norm[pl.ds(v, 1), :] = by_col[:, 0:128] + by_col[:, 128:256] + by_col[:, 256:384] + by_col[:, 384:512]
    for mode in range(2):
        slot_hot[mode] = slot_hot_t[mode].T
    members[pl.ds(FEAT, spare)] = jnp.zeros((spare, MEMBERS, COARSE), BF16)

    repeat = (
        lax.broadcasted_iota(jnp.int32, (SPREAD, MODES), 0) // GROUP
        == lax.broadcasted_iota(jnp.int32, (SPREAD, MODES), 1)
    ).astype(F32).astype(BF16)
    high = modes_ref[...].astype(BF16)
    low = (modes_ref[...] - high.astype(F32)).astype(BF16)
    modes_rep[...] = jnp.zeros_like(modes_rep)
    modes_rep[pl.ds(0, FEAT), :] = jnp.concatenate([dot(repeat, high), dot(repeat, low)], axis=0).T

    def mixer_step(i, carry):
        cut = (32, GROUP, 2 * SPREAD)
        rows = modes_rep[pl.ds(pl.multiple_of(i * 32, 32), 32), :]
        same = lax.broadcasted_iota(jnp.int32, cut, 1) == lax.broadcasted_iota(jnp.int32, cut, 2) % GROUP
        block = jnp.where(same, jnp.broadcast_to(rows[:, None, :], cut), 0.0).reshape(256, 2 * SPREAD)
        at = pl.ds(pl.multiple_of(i * 256, 256), 256)
        mixer[at, :] = block.astype(BF16)
        mixer_t[:, at] = block.T.astype(BF16)
        return carry

    lax.fori_loop(0, FEAT_PAD // 32, mixer_step, 0)

    for copy in index_copies:
        copy.wait_recv()
    lane = lax.broadcasted_iota(jnp.int32, (8, COARSE), 1)
    for mode in range(2):
        tables = [index_in[mode, p].astype(F32)[0:8] for p in range(8)]
        for b in range(4):
            halves = []
            for h in range(2):
                row = jnp.zeros((8, COARSE), F32)
                for g in range(4):
                    shift = (g - b) * CAP % COARSE
                    table = tables[h * 4 + g]
                    row = jnp.where(lane // CAP == g, pltpu.roll(table, shift, 1) if shift else table, row)
                halves.append(row[0:1])
            row = jnp.concatenate(halves, axis=1)
            hot = (lax.broadcasted_iota(jnp.int32, (COARSE, 8 * CAP), 0) + 1).astype(F32) == row
            hot = hot.astype(F32)
            place_t[mode, b] = hot.astype(BF16)
            place[mode, b] = hot.T.astype(BF16)
    load_members.wait()

    def contract(v):
        gathered_modes[...] = jnp.zeros_like(gathered_modes)

        def chunk(i, carry):
            field = coarse[pl.ds(pl.multiple_of(v * FEAT_PAD + i * STEP, STEP), STEP), :]
            cells = members[pl.ds(i * STEP, STEP)].astype(F32).reshape(STEP, GROUPS, GROUP, COARSE)
            product = cells * field[:, None, None, :]
            left = mixer_t[:, pl.ds(pl.multiple_of(i * STEP * GROUP, STEP * GROUP), STEP * GROUP)]
            for pair in range(GROUPS // 2):
                both = jnp.concatenate(
                    [product[:, 2 * pair + e].reshape(STEP * GROUP, COARSE) for e in range(2)], axis=1
                )
                top = both.astype(BF16)
                rest = (both - top.astype(F32)).astype(BF16)
                main = dot(left, top)
                gathered_modes[:, pair * 256 : (pair + 1) * 256] += (
                    main[0:SPREAD] + main[SPREAD:] + dot(left[0:SPREAD], rest)
                )
            return carry

        lax.fori_loop(0, FEAT_PAD // STEP, chunk, 0)
        for m in range(MODES):
            for g in range(GROUPS):
                control[pl.ds(v * ROWS + m * MEMBERS + g * GROUP, GROUP), :] = gathered_modes[
                    m * GROUP : (m + 1) * GROUP, g * COARSE : (g + 1) * COARSE
                ]

    def share_rows(v, t):
        return pl.ds(pl.multiple_of(v * ROWS + t * SHARE, 8), SHARE)

    def sum_start(v):
        copies = []
        for d in (2, 1, 3):
            t = (slot + d) % SLOTS
            copy = pltpu.make_async_remote_copy(
                src_ref=control.at[share_rows(v, t)],
                dst_ref=summed_in.at[v, d - 1],
                send_sem=sum_send.at[v, d - 1],
                recv_sem=sum_recv.at[v, d - 1],
                device_id={"slot": t},
                device_id_type=MESH,
            )
            copy.start()
            copies.append(copy)
        return copies

    def edges_start(v):
        cells = control[share_rows(v, slot), :]
        for d in range(3):
            cells = cells + summed_in[v, d]
        shares[v] = cells
        lane = lax.broadcasted_iota(jnp.int32, (40, COARSE), 1)
        east = jnp.zeros((40, COARSE), F32)
        west = jnp.zeros((40, COARSE), F32)
        for g in range(4):
            part = cells[g * 40 : (g + 1) * 40]
            mine = lane // 16 == g
            east = jnp.where(mine, pltpu.roll(part, 16 * g + 16, 1), east)
            west = jnp.where(mine, pltpu.roll(part, 16 * g, 1) if g else part, west)
        edge_out[v, 0] = east
        edge_out[v, 1] = west
        copies = []
        for side, p in ((0, (me + 1) % REGIONS), (1, (me + REGIONS - 1) % REGIONS)):
            copy = pltpu.make_async_remote_copy(
                src_ref=edge_out.at[v, side],
                dst_ref=edge_in.at[v, side],
                send_sem=edge_send.at[v, side],
                recv_sem=edge_recv.at[v, side],
                device_id={"region": p},
                device_id_type=MESH,
            )
            copy.start()
            copies.append(copy)
        return copies

    def smooth_share(v):
        cells = shares[v]
        lane = lax.broadcasted_iota(jnp.int32, (SHARE, COARSE), 1)
        west = jnp.concatenate([pltpu.roll(edge_in[v, 0], 112 - 16 * g, 1) for g in range(4)], axis=0)
        east = jnp.concatenate(
            [pltpu.roll(edge_in[v, 1], 128 - 16 * g, 1) if g else edge_in[v, 1] for g in range(4)], axis=0
        )
        once = smooth(cells, west, east)
        west = jnp.where(lane < LAT_ROWS, cells, west)
        east = jnp.where(lane >= COARSE - LAT_ROWS, cells, east)
        twice = smooth(once, smooth(west, west, west), smooth(east, east, east))
        norm[pl.ds(2 + v, 1), :] = jnp.sum(once * once, axis=0, keepdims=True)
        smooth_bits = twice.astype(BF16)
        gathered[v, slot] = smooth_bits
        copies = []
        for d in (2, 1, 3):
            copy = pltpu.make_async_remote_copy(
                src_ref=gathered.at[v, slot],
                dst_ref=gathered.at[v, slot],
                send_sem=share_send.at[v, d - 1],
                recv_sem=share_recv.at[v, d - 1],
                device_id={"slot": (slot + d) % SLOTS},
                device_id_type=MESH,
            )
            copy.start()
            copies.append(copy)
        return copies

    def expand(v):
        every = jnp.concatenate([gathered[v, t].astype(F32) for t in range(SLOTS)], axis=0)
        for g in range(GROUPS):
            cells = jnp.concatenate(
                [every[m * MEMBERS + g * GROUP : m * MEMBERS + (g + 1) * GROUP] for m in range(MODES)], axis=0
            ).astype(BF16)
            mode_cells[0:SPREAD, g * COARSE : (g + 1) * COARSE] = cells
            mode_cells[SPREAD:, g * COARSE : (g + 1) * COARSE] = cells

        def chunk(i, carry):
            left = mixer[pl.ds(pl.multiple_of(i * WIDE_STEP * GROUP, WIDE_STEP * GROUP), WIDE_STEP * GROUP), :]
            cells = members[pl.ds(i * WIDE_STEP, WIDE_STEP)].astype(F32).reshape(WIDE_STEP, GROUPS, GROUP, COARSE)
            sums = jnp.zeros((WIDE_STEP, GROUP, COARSE), F32)
            for pair in range(GROUPS // 2):
                mixed = dot(left, mode_cells[:, pair * 256 : (pair + 1) * 256])
                for e in range(2):
                    part = mixed[:, e * COARSE : (e + 1) * COARSE].reshape(WIDE_STEP, GROUP, COARSE)
                    sums = sums + cells[:, 2 * pair + e] * part
            at = pl.ds(pl.multiple_of(v * FEAT_PAD + i * WIDE_STEP, WIDE_STEP), WIDE_STEP)
            total[at, :] = jnp.sum(sums, axis=1)
            return carry

        lax.fori_loop(0, FEAT_PAD // WIDE_STEP, chunk, 0)

    def arrived(copies):
        for copy in copies:
            copy.wait_recv()

    def spread_start(piece):
        left, width, mode = BACK[piece]
        here = spot(mode)[1]
        spread_out[piece][...] = total[pl.ds(left, width), :].T.astype(BF16)
        copies = [
            push(
                spread_out[piece],
                spread_in[piece].at[here],
                spread_send.at[piece, j],
                spread_recv.at[piece, j],
                target,
            )
            for j, _, target in cross_peers(mode)
        ]
        spread_in[piece][here] = spread_out[piece][...]
        return copies

    def back_start(piece):
        _, width, mode = BACK[piece]
        here = spot(mode)[0] * 2 + core
        for b in range(4):
            rows = dot(place[mode, b], spread_in[piece][b])
            back[piece][:, b] = rows.astype(BF16).reshape(8, CAP, width)
        copies = [
            push(
                back[piece].at[there],
                home[piece].at[here],
                back_send.at[piece, j],
                back_recv.at[piece, j],
                target,
            )
            for j, there, target in line_peers(mode)
        ]
        home[piece][here] = back[piece][here]
        return copies

    def fine_rows(piece):
        left, width, mode = BACK[piece]
        source = home[piece][...].reshape(REGIONS * CAP, width)
        for q in range(4):
            cols = slice(q * 128, (q + 1) * 128)
            rows = dot(slot_hot[mode, pl.ds(q * 128, 128), :], source).T
            for v in range(2):
                first = max(left, v * FEAT_PAD)
                last = min(left + width, v * FEAT_PAD + FEAT)
                if first < last:
                    fine[v, first - v * FEAT_PAD : last - v * FEAT_PAD, cols] = rows[first - left : last - left]

    def store_start(v):
        copies = [pltpu.make_async_copy(fine.at[v], fine_hbm.at[:, v, :], load_sem.at[v])]
        for copy in copies:
            copy.start()
        return copies

    arrived(out_0)
    part_0 = part_start(0)
    arrived(out_1)
    part_1 = part_start(1)
    out_2 = out_start(2, out_0)
    out_3 = out_start(3, out_1)
    total[pl.ds(FEAT_PAD, FEAT_PAD), :] = jnp.zeros((FEAT_PAD, COARSE), F32)
    arrived(part_0)
    coarse_rows(0)
    arrived(part_1)
    coarse_rows(1)
    contract(0)
    sum_copies = sum_start(0)
    arrived(out_2)
    part_2 = part_start(2)
    arrived(out_3)
    part_3 = part_start(3)
    arrived(sum_copies)
    edge_copies = edges_start(0)
    arrived(edge_copies)
    share_copies = smooth_share(0)

    arrived(part_2)
    coarse_rows(2)
    arrived(part_3)
    coarse_rows(3)
    contract(1)
    sum_copies_b = sum_start(1)

    arrived(share_copies)
    expand(0)
    spread_0 = spread_start(0)
    spread_1 = spread_start(1)
    arrived(sum_copies_b)
    edge_copies_b = edges_start(1)
    arrived(edge_copies_b)
    share_copies_b = smooth_share(1)
    arrived(spread_0)
    back_0 = back_start(0)
    arrived(spread_1)
    back_1 = back_start(1)
    norm_copies = []
    for d in (2, 1, 3):
        copy = pltpu.make_async_remote_copy(
            src_ref=norm,
            dst_ref=norm_in.at[d - 1],
            send_sem=norm_send.at[d - 1],
            recv_sem=norm_recv.at[d - 1],
            device_id={"slot": (slot + d) % SLOTS},
            device_id_type=MESH,
        )
        copy.start()
        norm_copies.append(copy)
    arrived(share_copies_b)
    expand(1)
    spread_2 = spread_start(2)
    spread_3 = spread_start(3)
    spread_4 = spread_start(4)
    spread_5 = spread_start(5)
    arrived(norm_copies)
    norm_sum[...] = norm[...] + norm_in[0] + norm_in[1] + norm_in[2]
    last_copies = []
    for i, p in enumerate(partners):
        copy = pltpu.make_async_remote_copy(
            src_ref=norm_sum,
            dst_ref=norm_all.at[me],
            send_sem=last_send.at[i],
            recv_sem=last_recv.at[i],
            device_id={"region": p},
            device_id_type=MESH,
        )
        copy.start()
        last_copies.append(copy)
    norm_all[me] = norm_sum[...]

    arrived(spread_2)
    back_2 = back_start(2)
    arrived(spread_3)
    back_3 = back_start(3)
    arrived(spread_4)
    back_4 = back_start(4)
    arrived(spread_5)
    back_5 = back_start(5)

    arrived(back_0)
    fine_rows(0)
    arrived(back_1)
    fine_rows(1)
    arrived(last_copies)
    sums = jnp.sum(jnp.sum(norm_all[...], axis=0), axis=1, keepdims=True)
    squares = jnp.broadcast_to(sums, (8, COARSE))
    step = squares / (squares + pltpu.roll(squares, 6, 0))
    step_ref[...] = step
    arrived(back_2)
    fine_rows(2)
    stores = store_start(0)
    arrived(back_3)
    fine_rows(3)
    arrived(back_4)
    fine_rows(4)
    arrived(back_5)
    fine_rows(5)
    stores += store_start(1)
    for copies in (
        index_copies,
        out_2,
        out_3,
        part_0,
        part_1,
        part_2,
        part_3,
        sum_copies,
        sum_copies_b,
        edge_copies,
        edge_copies_b,
        share_copies,
        share_copies_b,
        norm_copies,
        last_copies,
        spread_0,
        spread_1,
        spread_2,
        spread_3,
        spread_4,
        spread_5,
        back_0,
        back_1,
        back_2,
        back_3,
        back_4,
        back_5,
    ):
        for copy in copies:
            copy.wait_send()
    for copy in stores:
        copy.wait()


def last_step(resid_ref, increment_ref, weight_ref, step_ref, product_ref, next_ref, length_ref):
    cut = (resid_ref.shape[0] // 8, 8, COARSE)
    row = lax.broadcasted_iota(jnp.int32, (8, COARSE), 0)
    step = jnp.where(row % 2 == 1, step_ref[1:2, :], step_ref[0:1, :])
    weight = weight_ref[:, 0:COARSE]
    for j in range(1, 4):
        weight = jnp.where(row // 2 == j, weight_ref[:, j * COARSE : (j + 1) * COARSE], weight)
    for v in range(2):
        length_ref[v] = jnp.max(step_ref[v : v + 1, :])
    resid = resid_ref[...].reshape(cut)
    product = resid + increment_ref[...].reshape(cut) * weight[None]
    product_ref[...] = product.reshape(resid_ref.shape)
    next_ref[...] = (resid - step[None] * product).reshape(resid_ref.shape)


def by_lanes(fields):
    return fields.reshape(FEAT, 2, 4, COARSE).transpose(0, 2, 1, 3).reshape(FEAT * 8, COARSE)


def by_fields(rows):
    return rows.reshape(FEAT, 4, 2, COARSE).transpose(2, 0, 1, 3).reshape(1, 2, FEAT, FINE)


def per_device(residual, perturb, vertical_modes, column_weight, owner_table, column_map):
    vmem, dma = pltpu.VMEM, pltpu.SemaphoreType.DMA
    resid_part = residual[0].transpose(1, 0, 2)
    weight = column_weight.reshape(1, FINE)
    whole = pl.BlockSpec(memory_space=pltpu.VMEM)
    anywhere = pl.BlockSpec(memory_space=pl.ANY)
    n = len(HOPS)
    increment, step = pl.pallas_call(
        kernel,
        out_shape=(
            jax.ShapeDtypeStruct((FEAT, 2, FINE), F32),
            jax.ShapeDtypeStruct((8, COARSE), F32),
        ),
        in_specs=[whole] * 4 + [anywhere] * 2,
        out_specs=(anywhere, whole),
        scratch_shapes=[
            vmem((2, FEAT, FINE), F32),
            vmem((FEAT_PAD, MEMBERS, COARSE), BF16),
            vmem((WIDE, FINE), F32),
            vmem((FINE, WIDE), BF16),
            vmem((2, REGIONS * CAP, FINE), BF16),
            vmem((2, FINE, REGIONS * CAP), BF16),
            vmem((2, 8, 16, COARSE), BF16),
            vmem((2, 8, 16, COARSE), BF16),
            vmem((2, 4, 8 * CAP, COARSE), BF16),
            vmem((2, 4, COARSE, 8 * CAP), BF16),
            [vmem((8, 4, CAP, width), BF16) for _, width, _ in OUT],
            [vmem((4, 8, CAP, width), BF16) for _, width, _ in OUT],
            [vmem((4, COARSE, width), BF16) for _, width, _ in OUT],
            [vmem((4, COARSE, width), BF16) for _, width, _ in OUT],
            vmem((WIDE, COARSE), F32),
            vmem((FEAT_PAD, 2 * SPREAD), F32),
            vmem((FEAT_PAD * GROUP, 2 * SPREAD), BF16),
            vmem((2 * SPREAD, FEAT_PAD * GROUP), BF16),
            vmem((SPREAD, GROUPS * COARSE), F32),
            vmem((2 * SPREAD, GROUPS * COARSE), BF16),
            vmem((2 * ROWS, COARSE), F32),
            vmem((2, SLOTS - 1, SHARE, COARSE), F32),
            vmem((2, 2, 40, COARSE), F32),
            vmem((2, 2, 40, COARSE), F32),
            vmem((2, SHARE, COARSE), F32),
            vmem((2, SLOTS, SHARE, COARSE), BF16),
            vmem((WIDE, COARSE), F32),
            [vmem((COARSE, width), BF16) for _, width, _ in BACK],
            [vmem((4, COARSE, width), BF16) for _, width, _ in BACK],
            [vmem((8, 4, CAP, width), BF16) for _, width, _ in BACK],
            [vmem((8, 4, CAP, width), BF16) for _, width, _ in BACK],
            vmem((2, FEAT, FINE), F32),
            vmem((8, COARSE), F32),
            vmem((SLOTS - 1, 8, COARSE), F32),
            vmem((8, COARSE), F32),
            vmem((REGIONS, 8, COARSE), F32),
            dma((3,)),
            *[dma((rows, cols)) for rows, cols in ((2, 7), (4, 7), (4, 3), (6, 3), (6, 7)) for _ in range(2)],
            dma((2, 3)),
            dma((2, 3)),
            dma((2, 2)),
            dma((2, 2)),
            dma((2, 3)),
            dma((2, 3)),
            dma((3,)),
            dma((3,)),
            dma((n,)),
            dma((n,)),
        ],
        compiler_params=pltpu.CompilerParams(
            collective_id=0, has_side_effects=True, vmem_limit_bytes=60 * 2**20
        ),
        name="hessian",
    )(
        owner_table.reshape(1, REGIONS * FINE),
        column_map.reshape(1, REGIONS * FINE),
        weight,
        vertical_modes.T,
        resid_part,
        perturb[0].transpose(1, 0, 2),
    )
    rows = FEAT // 5 * 8
    block = pl.BlockSpec((rows, COARSE), lambda i: (i, 0))
    small = pl.BlockSpec((8, COARSE), lambda i: (0, 0))
    product, next_residual, step_length = pl.pallas_call(
        last_step,
        grid=(5,),
        out_shape=(jax.ShapeDtypeStruct((FEAT * 8, COARSE), F32),) * 2 + (jax.ShapeDtypeStruct((2,), F32),),
        in_specs=[block, block, pl.BlockSpec((1, FINE), lambda i: (0, 0)), small],
        out_specs=(block, block, pl.BlockSpec(memory_space=pltpu.SMEM)),
        name="last_step",
    )(
        by_lanes(resid_part),
        by_lanes(increment),
        weight,
        step,
    )
    return (by_fields(product), step_length, by_fields(next_residual))


def solution(mesh):
    in_specs = (
        P("slot", None, None, "region"),
        P("slot", None, None, "region"),
        P(),
        P("region"),
        P(),
        P(),
    )
    out_specs = (P("slot", None, None, "region"), P(), P("slot", None, None, "region"))
    return jax.shard_map(
        per_device, mesh=mesh, in_specs=in_specs, out_specs=out_specs, check_vma=False
    )
```
